32 devices in a mesh: tok: 2 (over y), feat: 16 (over z, x, core).
Axes of the slice: x: 2, y: 2, z: 4, core: 2. Of those that a mesh axis runs over, the one named last changes fastest.
Arguments:
- tokens: bfloat16 [256, 4096], P('tok', 'feat'), may hold values from -6 to 6
- seq_lengths: int32 [4], replicated, may hold values from 1 to 64, 128 in all
- in_exponents: int32 [4096], replicated, may hold values from -1 to 1
- hidden_exponents: int32 [16384], P('feat'), may hold values from -2 to 0
- gateup_blocks: int32 [128, 16], P('feat'), may hold values from 0 to 31, as said below
- down_blocks: int32 [128, 16], P('feat'), may hold values from 0 to 31, as said below
- gate_values: bfloat16 [128, 16, 128, 128], P('feat', 'tok'), may hold values from -0.125 to 0.125
- up_values: bfloat16 [128, 16, 128, 128], P('feat', 'tok'), may hold values from -0.125 to 0.125
- down_values: bfloat16 [128, 16, 128, 128], P('feat', 'tok'), may hold values from -0.25 to 0.25
Outputs:
- ffn_output: bfloat16 [256, 4096], P('tok', 'feat')
The draws below stay inside these ranges and needn't reach their ends.
Inputs may be any that keep to these rules, and one draw needn't show every extreme that they name: `seq_lengths`: the lengths add up to 128; sequence q fills the token slots from q * 64 on, the rest of its 64 slots is empty. `gateup_blocks`: each row holds 16 different block numbers in rising order. `down_blocks`: each row holds 16 different block numbers in rising order.
All inputs are finite; a program needn't handle non-finite values.
Results may differ from the reference program's by a relative error of at most 0.0057.
Values may be sent and summed in bfloat16 or wider, within the bound.
A program may use at most 128 MiB of HBM per device.

```python
import math
import jax
import jax.numpy as jnp
import numpy as np
from jax import lax

D = 4096
FF = 16384
BLOCK_SIDE = 128
NNZ = 16
TIME_STEPS = 4
SLOT = 64
NSEQ = 4
TOKEN_SLOTS = 256
LIVE = 128
HIDDEN_BLOCKS = 128
NBLK_D = 32


def pick_blocks(seed_key):
    scores = jax.random.randint(seed_key, (HIDDEN_BLOCKS, NBLK_D), 0, 1048576, dtype=jnp.int32) * NBLK_D + jnp.arange(NBLK_D, dtype=jnp.int32)[None, :]
    ranking = jnp.argsort(scores, axis=1)[:, :NNZ]
    return jnp.sort(ranking, axis=1).astype(jnp.int32)


def draw_gateup_blocks(key, part):
    return pick_blocks(jax.random.fold_in(key, 11))


def draw_down_blocks(key, part):
    return pick_blocks(jax.random.fold_in(key, 23))


def plant(values, rng, smallest, top_value):
    longest = values.shape.index(max(values.shape))
    spots = []
    for shift in (0, 1):
        where = [jax.random.randint(jax.random.fold_in(rng, axis), (), 0, length) for axis, length in enumerate(values.shape)]
        where[longest] = (where[longest] + shift) % values.shape[longest]
        spots.append(tuple(where))
    return values.at[spots[0]].set(smallest).at[spots[1]].set(top_value)


def levels(rng, dims, split, least, top_value):
    factor_of, own = 1.0, jax.random.fold_in(rng, 6)
    for dim, parts in split:
        heights = jnp.exp(jax.random.uniform(jax.random.fold_in(own, dim), (parts,), jnp.float32, least / len(split), top_value / len(split)))
        factor_of = factor_of * jnp.repeat(heights, dims[dim] // parts).reshape([-1 if axis == dim else 1 for axis in range(len(dims))])
    return factor_of


def split_up(count, total, most, lean):
    loads = [(1 << 20) // math.isqrt(rank ** lean) + 1 for rank in range(2, count + 1)]
    surplus, given = total - most - (count - 1), [1] * (count - 1)
    while surplus > 0:
        movable = [i for i in range(count - 1) if given[i] < most]
        mass, remaining = sum([loads[i] for i in movable]), surplus
        for i in movable:
            more = min(most - given[i], max(1, remaining * loads[i] // mass), surplus)
            given[i] = given[i] + more
            surplus = surplus - more
    return np.array([most] + given)


def ragged(key, count, total, reach, slope):
    if count == 2:
        one = jax.random.randint(key, (), max(1, total - reach), min(reach, total - 1) + 1)
        return jnp.stack([one, total - one])
    lengths = jnp.asarray(split_up(count, total, reach, slope), jnp.int32)
    couples = (count - 1) // 2
    source_of, taker = lengths[1:1 + 2 * couples:2], lengths[2:2 + 2 * couples:2]
    room = jnp.minimum(source_of - 1, reach - taker)
    passed = jax.random.randint(jax.random.fold_in(key, 1), (couples,), 0, 1 << 20) % (room + 1)
    lengths = lengths.at[1:1 + 2 * couples:2].set(source_of - passed).at[2:2 + 2 * couples:2].set(taker + passed)
    return lengths[jax.random.permutation(jax.random.fold_in(key, 2), count)]


def noise(key, shape, scale, limit, shards=(), kind=jnp.bfloat16):
    entries = scale * jax.random.normal(key, shape, jnp.float32)
    if shards:
        entries = entries * levels(key, shape, shards, -0.22, 0.18)
    return jnp.clip(entries, -limit, limit).astype(kind)


def setup_inputs(seed: int = 0) -> dict:
    arg_keys = jax.random.split(jax.random.key(seed), 10)
    tokens = noise(arg_keys[0], (TOKEN_SLOTS, D), 1.0, 6.0, ((0, 2), (1, 16)))
    seq_lengths = ragged(arg_keys[1], NSEQ, LIVE, SLOT, 2).astype(jnp.int32)
    in_exponents = plant(jax.random.randint(arg_keys[2], (D,), -1, 2), jax.random.fold_in(arg_keys[2], 1), -1, 1).astype(jnp.int32)
    hidden_exponents = plant(jax.random.randint(arg_keys[3], (FF,), -2, 1), jax.random.fold_in(arg_keys[3], 1), -2, 0).astype(jnp.int32)
    gateup_blocks = draw_gateup_blocks(jax.random.fold_in(arg_keys[9], 71), 0)
    down_blocks = draw_down_blocks(jax.random.fold_in(arg_keys[9], 71), 0)
    gate_values = noise(arg_keys[6], (HIDDEN_BLOCKS, NNZ, BLOCK_SIDE, BLOCK_SIDE), (NNZ * BLOCK_SIDE) ** -0.5, 0.125, ((0, 16), (1, 2)))
    up_values = noise(arg_keys[7], (HIDDEN_BLOCKS, NNZ, BLOCK_SIDE, BLOCK_SIDE), (NNZ * BLOCK_SIDE) ** -0.5, 0.125, ((0, 16), (1, 2)))
    down_values = noise(arg_keys[8], (HIDDEN_BLOCKS, NNZ, BLOCK_SIDE, BLOCK_SIDE), (FF * NNZ * BLOCK_SIDE // (16 * D)) ** -0.5, 0.25, ((0, 16), (1, 2)))
    return {"tokens": tokens, "seq_lengths": seq_lengths, "in_exponents": in_exponents, "hidden_exponents": hidden_exponents, "gateup_blocks": gateup_blocks, "down_blocks": down_blocks, "gate_values": gate_values, "up_values": up_values, "down_values": down_values}


def walsh_rows(values):
    row_count, model_width = values.shape
    stride_size = 1
    while stride_size < model_width:
        shaped = values.reshape(row_count, model_width // (2 * stride_size), 2, stride_size)
        lower_half = shaped[:, :, 0, :]
        upper_half = shaped[:, :, 1, :]
        values = jnp.stack([lower_half + upper_half, lower_half - upper_half], axis=2).reshape(row_count, model_width)
        stride_size = stride_size * 2
    return values

def pair_products(spikes, blocks, gate_values, up_values):

    def single_block(operands):
        index_row, gate_block, up_block = operands
        picked = jnp.take(spikes, index_row.astype(jnp.int32), axis=1).astype(jnp.float32)
        gate_sum = jnp.einsum('nkb,kbc->nc', picked, gate_block.astype(jnp.float32))
        upward = jnp.einsum('nkb,kbc->nc', picked, up_block.astype(jnp.float32))
        return (gate_sum, upward)
    gate_sum, upward = lax.map(single_block, (blocks, gate_values, up_values))
    row_count = spikes.shape[0]
    gate_sum = jnp.transpose(gate_sum, (1, 0, 2)).reshape(row_count, FF)
    upward = jnp.transpose(upward, (1, 0, 2)).reshape(row_count, FF)
    return (gate_sum, upward)

def reference(tokens, seq_lengths, in_exponents, hidden_exponents, gateup_blocks, down_blocks, gate_values, up_values, down_values):
    rotated = (walsh_rows(tokens.astype(jnp.float32)) * (1.0 / math.sqrt(D))).astype(jnp.bfloat16)
    in_limit = jnp.exp2(in_exponents.astype(jnp.float32))
    hidden_limit = jnp.exp2(hidden_exponents.astype(jnp.float32))
    v_in = jnp.zeros((TOKEN_SLOTS, D), jnp.float32)
    v_hidden = jnp.zeros((TOKEN_SLOTS, FF), jnp.float32)
    spike_count_sum = jnp.zeros((TOKEN_SLOTS, FF), jnp.float32)
    for step_index in range(TIME_STEPS):
        v_in = v_in + rotated.astype(jnp.float32)
        spike_in = jnp.clip(v_in, -in_limit, in_limit).astype(jnp.bfloat16)
        v_in = v_in - spike_in.astype(jnp.float32)
        gate_sum, upward = pair_products(spike_in.reshape(TOKEN_SLOTS, NBLK_D, BLOCK_SIDE), gateup_blocks, gate_values, up_values)
        v_hidden = v_hidden + jax.nn.silu(gate_sum) * upward
        spike_hidden = jnp.clip(v_hidden, -hidden_limit, hidden_limit)
        v_hidden = v_hidden - spike_hidden
        spike_count_sum = spike_count_sum + spike_hidden
    spiking_rate = (spike_count_sum / TIME_STEPS).astype(jnp.bfloat16)
    each_block_result = jnp.transpose(spiking_rate.reshape(TOKEN_SLOTS, HIDDEN_BLOCKS, BLOCK_SIDE), (1, 0, 2))

    def add_block(accumulated, operands):
        index_row, down_block, rate_block = operands
        contribution = jnp.einsum('nb,kbc->nkc', rate_block.astype(jnp.float32), down_block.astype(jnp.float32))
        return (accumulated.at[:, index_row.astype(jnp.int32)].add(contribution), None)
    accumulated, unused = lax.scan(add_block, jnp.zeros((TOKEN_SLOTS, NBLK_D, BLOCK_SIDE), jnp.float32), (down_blocks, down_values, each_block_result))
    slot_ids = jnp.arange(TOKEN_SLOTS, dtype=jnp.int32)
    seq_of = slot_ids // SLOT
    position = slot_ids % SLOT
    live_slot = position < jnp.take(seq_lengths, seq_of)
    return jnp.where(live_slot[:, None], accumulated.reshape(TOKEN_SLOTS, D), 0.0).astype(jnp.bfloat16)
```

```python
import math

import jax
import jax.numpy as jnp
import numpy as np
from jax import lax
from jax.experimental import pallas as pl
from jax.experimental.pallas import tpu as pltpu
from jax.sharding import PartitionSpec as P

SEQS_DEV = 2
MESH_ID = pl.DeviceIdType.MESH
F32 = jnp.float32
BF16 = jnp.bfloat16


def slot_target(lengths, slots, seq_width):
    seq = slots // seq_width
    position = slots % seq_width
    start = jnp.zeros_like(slots)
    length = jnp.zeros_like(slots)
    running = 0
    for q, length_q in enumerate(lengths):
        here = seq == q
        start = jnp.where(here, running, start)
        length = jnp.where(here, length_q, length)
        running = running + length_q
    return jnp.where(position < length, start + position, -1)


def body(
    lengths_ref,
    gateup_ref,
    slot_of_ref,
    tok_ref,
    in_exp_ref,
    hid_exp_ref,
    sign_ref,
    gate_hbm,
    up_hbm,
    down_hbm,
    out_ref,
    gate,
    up,
    down,
    peer_tok,
    all_tok,
    mixed,
    in_limit,
    spikes,
    snd_gu,
    rcv_gu,
    rate,
    snd_c,
    rcv_c,
    snd_x,
    rcv_x,
    acc,
    snd_y,
    rcv_y,
    snd_z,
    rcv_z,
    final,
    w_sem,
    raw_s,
    raw_r,
    agz_s,
    agz_r,
    agx_s,
    agx_r,
    agc_s,
    agc_r,
    gu_s,
    gu_r,
    rt_s,
    rt_r,
    c_s,
    c_r,
    x_s,
    x_r,
    y_s,
    y_r,
    z_s,
    z_r,
    fin_s,
    fin_r,
):
    t = lax.axis_index("tok")
    f = lax.axis_index("feat")
    z = f // 4
    x = (f // 2) % 2
    c = f % 2
    slots, width = tok_ref.shape
    live = slots
    half = live // 2
    side = slots // SEQS_DEV
    columns = rate.shape[0]
    mine = columns // 2
    kk = gateup_ref.shape[1] // 2

    dev_y = (1 - t, f)
    dev_c = (t, f + 1 - 2 * c)
    dev_x = (t, f + 2 - 4 * x)

    def z_at(d):
        return lax.rem(z + d, 4)

    def dev_z(d):
        return (t, z_at(d) * 4 + x * 2 + c)

    def chunk(zz, xx, cc):
        return zz * 4 + xx * 2 + cc

    def send(src, dst, ssem, rsem, dev):
        return pltpu.make_async_remote_copy(
            src_ref=src,
            dst_ref=dst,
            send_sem=ssem,
            recv_sem=rsem,
            device_id=dev,
            device_id_type=MESH_ID,
        )

    w_copies = [
        pltpu.make_async_copy(gate_hbm, gate, w_sem.at[0]),
        pltpu.make_async_copy(up_hbm, up, w_sem.at[1]),
        pltpu.make_async_copy(down_hbm, down.at[:, pl.ds(1, kk)], w_sem.at[2]),
    ]
    for copy in w_copies:
        copy.start()

    barrier = pltpu.get_barrier_semaphore()
    partners = [dev_y, dev_c, dev_x, dev_z(1), dev_z(2), dev_z(3)]
    for dev in partners:
        pl.semaphore_signal(barrier, inc=1, device_id=dev, device_id_type=MESH_ID)
    pl.semaphore_wait(barrier, len(partners))

    raw = send(tok_ref, peer_tok, raw_s.at[0], raw_r.at[0], dev_y)
    raw.start()
    down[:, pl.ds(0, 1)] = jnp.zeros((columns, 1) + down.shape[2:], BF16)
    in_limit[...] = jnp.exp2(in_exp_ref[...].astype(F32)).astype(BF16).astype(F32)
    lengths = [lengths_ref[q] for q in range(lengths_ref.shape[0])]
    rows = lax.broadcasted_iota(jnp.int32, (live, slots), 0)
    lane_slots = lax.broadcasted_iota(jnp.int32, (live, slots), 1)

    def pick(group):
        target = slot_target(lengths, lane_slots + group * slots, side)
        return jnp.where(target == rows, 1.0, 0.0).astype(BF16)

    own_rows = jnp.dot(pick(t), tok_ref[...], preferred_element_type=F32)
    other_pick = pick(1 - t)
    raw.wait_recv()
    other_rows = jnp.dot(other_pick, peer_tok[...], preferred_element_type=F32)
    all_tok[f] = (own_rows + other_rows).astype(BF16)

    sent = [raw]

    def start(copy):
        copy.start()
        sent.append(copy)
        return copy

    def rotate_low(g):
        mixed[g] = jnp.dot(all_tok[g], sign_ref[...], preferred_element_type=F32)

    def forward_x(d, g):
        return start(send(all_tok.at[g], all_tok.at[g], agx_s.at[d], agx_r.at[d], dev_x))

    def forward_c(d, g):
        return start(send(all_tok.at[g], all_tok.at[g], agc_s.at[d], agc_r.at[d], dev_c))

    z_copies = [
        start(send(all_tok.at[f], all_tok.at[f], agz_s.at[d - 1], agz_r.at[d - 1], dev_z(d)))
        for d in (1, 2, 3)
    ]
    x_copies = [forward_x(0, f)]
    c_copies = [forward_c(0, f)]
    rotate_low(f)
    for d in (1, 3, 2):
        z_copies[d - 1].wait_recv()
        g = chunk(z_at(4 - d), x, c)
        x_copies.append(forward_x(d, g))
        c_copies.append(forward_c(d, g))
        rotate_low(g)
    for i, d in enumerate((0, 1, 3, 2)):
        x_copies[i].wait_recv()
        g = chunk(z_at(4 - d), 1 - x, c)
        c_copies.append(forward_c(4 + d, g))
        rotate_low(g)
    for i, d in enumerate((0, 1, 3, 2)):
        c_copies[i].wait_recv()
        rotate_low(chunk(z_at(4 - d), x, 1 - c))
    for i, d in enumerate((0, 1, 3, 2)):
        c_copies[4 + i].wait_recv()
        rotate_low(chunk(z_at(4 - d), 1 - x, 1 - c))

    chunks = mixed.shape[0]
    scale = 1.0 / math.sqrt(chunks * width)
    parts = width // 128

    def rotate_high(r, carry):
        at = pl.ds(pl.multiple_of(r * 16, 16), 16)
        for h in range(parts):
            vals = [mixed[i, at, pl.ds(h * 128, 128)] for i in range(chunks)]
            bit = 1
            while bit < chunks:
                nxt = list(vals)
                for i in range(chunks):
                    if not i & bit:
                        nxt[i] = vals[i] + vals[i | bit]
                        nxt[i | bit] = vals[i] - vals[i | bit]
                vals = nxt
                bit *= 2
            for i in range(chunks):
                n = parts * i + h
                limit = in_limit[pl.ds(n, 1), :]
                rotated = (vals[i] * scale).astype(BF16).astype(F32)
                spikes[n, at, :] = jnp.minimum(jnp.maximum(rotated, -limit), limit).astype(BF16)
        return carry

    lax.fori_loop(0, live // 16, rotate_high, 0)

    w_copies[0].wait()
    w_copies[1].wait()

    def pair_sums(j):
        lhs = jnp.concatenate([spikes[gateup_ref[j, t * kk + k]] for k in range(kk)], axis=1)
        rhs = jnp.concatenate([gate[j], up[j]], axis=1)
        return jnp.dot(lhs, rhs, preferred_element_type=F32)

    def gu_copy(i):
        return send(snd_gu.at[i], rcv_gu.at[i], gu_s.at[i], gu_r.at[i], dev_y)

    def rate_copy(i):
        j = t * mine + i
        return send(rate.at[j], rate.at[j], rt_s.at[i], rt_r.at[i], dev_y)

    def give(i, carry):
        snd_gu[i] = pair_sums((1 - t) * mine + i).astype(BF16)
        gu_copy(i).start()
        return carry

    def take(i, carry):
        j = t * mine + i
        own = pair_sums(j)
        gu_copy(i).wait_recv()
        total = own + rcv_gu[i].astype(F32)
        gate_sum = total[:, :128]
        current = gate_sum / (1.0 + jnp.exp(-gate_sum)) * total[:, 128:]
        limit = jnp.exp2(hid_exp_ref[pl.ds(j, 1), :].astype(F32)).astype(BF16).astype(F32)
        rate[j] = jnp.minimum(jnp.maximum(current, -limit), limit).astype(BF16)
        rate_copy(i).start()
        return carry

    lax.fori_loop(0, mine, give, 0)
    lax.fori_loop(0, mine, take, 0)
    w_copies[2].wait()
    for i in range(mine):
        rate_copy(i).wait_recv()

    def down_chunk(g):
        lhs = jnp.concatenate([rate[j] for j in range(columns)], axis=1)
        cols = []
        for h in range(parts):
            n = g * parts + h
            cols.append(
                jnp.concatenate([down[j, slot_of_ref[j, n]] for j in range(columns)], axis=0)
            )
        return jnp.dot(lhs, jnp.concatenate(cols, axis=1), preferred_element_type=F32)

    def core_copy(i):
        return send(snd_c.at[i], rcv_c.at[i], c_s.at[i], c_r.at[i], dev_c)

    def x_copy(i):
        return send(snd_x.at[i], rcv_x.at[i], x_s.at[i], x_r.at[i], dev_x)

    def y_copy(i):
        return send(snd_y.at[i], rcv_y.at[i], y_s.at[i], y_r.at[i], dev_y)

    def give_core_far(i, carry):
        snd_c[i] = down_chunk(chunk(i, 1 - x, 1 - c)).astype(BF16)
        core_copy(i).start()
        return carry

    def give_core_near(i, carry):
        snd_c[4 + i] = down_chunk(chunk(i, x, 1 - c)).astype(BF16)
        core_copy(4 + i).start()
        return carry

    def give_x(i, carry):
        own = down_chunk(chunk(i, 1 - x, c))
        core_copy(i).wait_recv()
        snd_x[i] = (own + rcv_c[i].astype(F32)).astype(BF16)
        x_copy(i).start()
        return carry

    def keep(i, carry):
        own = down_chunk(chunk(i, x, c))
        core_copy(4 + i).wait_recv()
        acc[i] = own + rcv_c[4 + i].astype(F32)
        return carry

    my_rows = pl.ds(pl.multiple_of(t * half, half), half)
    peer_rows = pl.ds(pl.multiple_of((1 - t) * half, half), half)

    def give_y(i, carry):
        x_copy(i).wait_recv()
        snd_y[i] = (acc[i, peer_rows, :] + rcv_x[i, peer_rows, :].astype(F32)).astype(BF16)
        y_copy(i).start()
        return carry

    lax.fori_loop(0, 4, give_core_far, 0)
    lax.fori_loop(0, 4, give_x, 0)
    lax.fori_loop(0, 4, give_core_near, 0)
    lax.fori_loop(0, 4, keep, 0)
    lax.fori_loop(0, 4, give_y, 0)

    def own_sum(i):
        y_copy(i).wait_recv()
        return (
            acc[i, my_rows, :] + rcv_x[i, my_rows, :].astype(F32) + rcv_y[i].astype(F32)
        )

    zs = []
    for d in (2, 1, 3):
        snd_z[d - 1] = own_sum(z_at(d)).astype(BF16)
        zs.append(
            start(send(snd_z.at[d - 1], rcv_z.at[d - 1], z_s.at[d - 1], z_r.at[d - 1], dev_z(d)))
        )
    total = own_sum(z)
    for copy, d in zip(zs, (2, 1, 3)):
        copy.wait_recv()
        total = total + rcv_z[d - 1].astype(F32)
    final[my_rows, :] = total.astype(BF16)
    fin = start(send(final.at[my_rows], final.at[my_rows], fin_s.at[0], fin_r.at[0], dev_y))
    slot_rows = lax.broadcasted_iota(jnp.int32, (slots, live), 0) + t * slots
    live_lanes = lax.broadcasted_iota(jnp.int32, (slots, live), 1)
    place = jnp.where(slot_target(lengths, slot_rows, side) == live_lanes, 1.0, 0.0).astype(BF16)
    fin.wait_recv()
    out_ref[...] = jnp.dot(place, final[...], preferred_element_type=F32).astype(BF16)

    for copy in sent:
        copy.wait_send()
    for i in range(mine):
        gu_copy(i).wait_send()
        rate_copy(i).wait_send()
    for i in range(8):
        core_copy(i).wait_send()
    for i in range(4):
        x_copy(i).wait_send()
        y_copy(i).wait_send()


def sign_matrix(size):
    index = np.arange(size)
    shared = index[:, None] & index[None, :]
    parity = np.zeros_like(shared)
    for bit_number in range(max(1, (size - 1).bit_length())):
        parity ^= (shared >> bit_number) & 1
    return 1 - 2 * parity


def local_kernel(
    tokens,
    seq_lengths,
    in_exponents,
    hidden_exponents,
    gateup_blocks,
    down_blocks,
    gate_values,
    up_values,
    down_values,
):
    slots, width = tokens.shape
    columns, kk, side, _ = gate_values.shape
    model_width = in_exponents.shape[0]
    blocks = model_width // side
    chunks = model_width // width
    mine = columns // 2
    half = slots // 2
    t = lax.axis_index("tok")
    held = lax.dynamic_slice_in_dim(down_blocks, t * kk, kk, axis=1)
    match = held[:, :, None] == jnp.arange(blocks, dtype=jnp.int32)[None, None, :]
    number = jnp.arange(1, kk + 1, dtype=jnp.int32)[None, :, None]
    slot_of = jnp.sum(jnp.where(match, number, 0), axis=1)

    vmem = pl.BlockSpec(memory_space=pltpu.VMEM)
    smem = pl.BlockSpec(memory_space=pltpu.SMEM)
    anywhere = pl.BlockSpec(memory_space=pl.ANY)
    dma = lambda n: pltpu.SemaphoreType.DMA((n,))
    buf = lambda *shape: pltpu.VMEM(shape, BF16)
    return pl.pallas_call(
        body,
        out_shape=jax.ShapeDtypeStruct((slots, width), BF16),
        in_specs=[smem] * 3 + [vmem] * 4 + [anywhere] * 3,
        out_specs=vmem,
        scratch_shapes=[
            buf(columns, kk * side, side),
            buf(columns, kk * side, side),
            buf(columns, kk + 1, side, side),
            buf(slots, width),
            buf(chunks, slots, width),
            pltpu.VMEM((chunks, slots, width), F32),
            pltpu.VMEM((blocks, side), F32),
            buf(blocks, slots, side),
            buf(mine, slots, 2 * side),
            buf(mine, slots, 2 * side),
            buf(columns, slots, side),
            buf(8, slots, width),
            buf(8, slots, width),
            buf(4, slots, width),
            buf(4, slots, width),
            pltpu.VMEM((4, slots, width), F32),
            buf(4, half, width),
            buf(4, half, width),
            buf(3, half, width),
            buf(3, half, width),
            buf(slots, width),
            dma(3),
            dma(1),
            dma(1),
            dma(3),
            dma(3),
            dma(4),
            dma(4),
            dma(8),
            dma(8),
            dma(mine),
            dma(mine),
            dma(mine),
            dma(mine),
            dma(8),
            dma(8),
            dma(4),
            dma(4),
            dma(4),
            dma(4),
            dma(3),
            dma(3),
            dma(1),
            dma(1),
        ],
        compiler_params=pltpu.CompilerParams(
            collective_id=0, has_side_effects=True, vmem_limit_bytes=40 * 1024 * 1024
        ),
        name="spiking_ffn",
    )(
        seq_lengths,
        gateup_blocks,
        slot_of,
        tokens,
        in_exponents.reshape(blocks, side),
        hidden_exponents.reshape(columns, side),
        jnp.asarray(sign_matrix(width), BF16),
        gate_values.reshape(columns, kk * side, side),
        up_values.reshape(columns, kk * side, side),
        down_values,
    )


def partner_2(value, axis, stride):
    mask = 2**stride
    pairs = [(source, source ^ mask) for source in range(lax.axis_size(axis))]
    return lax.ppermute(value, axis, pairs)


def sign_table(order_size, value_type):
    indices = jnp.arange(order_size, dtype=jnp.int32)
    shared = indices[:, None] & indices[None, :]
    parity = jnp.zeros((order_size, order_size), jnp.int32)
    for bit_number in range(max(1, (order_size - 1).bit_length())):
        parity = parity ^ shared >> bit_number & 1
    return (1 - 2 * parity).astype(value_type)


def local_general(
    tokens,
    seq_lengths,
    in_exponents,
    hidden_exponents,
    gateup_blocks,
    down_blocks,
    gate_values,
    up_values,
    down_values,
):
    slot_count, feat_local = tokens.shape
    model_width = in_exponents.shape[0]
    seq_width = slot_count // SEQS_DEV
    tok_index = lax.axis_index("tok")
    seq_count = seq_lengths.shape[0]
    earlier = jnp.tril(jnp.ones((seq_count, seq_count), jnp.int32))
    seq_ends = jnp.sum(earlier * seq_lengths[None, :], axis=1)
    seq_starts = seq_ends - seq_lengths
    seq_ids = jnp.arange(seq_lengths.shape[0], dtype=jnp.int32)
    slot_ids = jnp.arange(slot_count, dtype=jnp.int32)
    seq_of = tok_index * SEQS_DEV + slot_ids // seq_width
    position = slot_ids % seq_width
    same_seq = seq_of[:, None] == seq_ids[None, :]
    length_of = jnp.sum(jnp.where(same_seq, seq_lengths[None, :], 0), axis=1)
    start_of = jnp.sum(jnp.where(same_seq, seq_starts[None, :], 0), axis=1)
    live_slot = position < length_of
    pooled = lax.all_gather(tokens, "tok", axis=0, tiled=True)
    wanted = tok_index * seq_width + jnp.arange(seq_width, dtype=jnp.int32)
    owner_seq = jnp.sum((seq_ends[None, :] <= wanted[:, None]).astype(jnp.int32), axis=1)
    owner_match = owner_seq[:, None] == seq_ids[None, :]
    offset = wanted - jnp.sum(jnp.where(owner_match, seq_starts[None, :], 0), axis=1)
    picked_slot = owner_seq * seq_width + offset
    pooled_slots = jnp.arange(pooled.shape[0], dtype=jnp.int32)
    picker = (picked_slot[:, None] == pooled_slots[None, :]).astype(jnp.bfloat16)
    picked = jnp.dot(picker, pooled, preferred_element_type=jnp.float32).astype(jnp.bfloat16)
    row_count = picked.shape[0]
    rotation_scale = 1.0 / math.sqrt(model_width)
    mixed_part = jnp.dot(
        picked, sign_table(feat_local, jnp.bfloat16), preferred_element_type=jnp.float32
    )
    feat_index = lax.axis_index("feat")
    for bit_number in range(lax.axis_size("feat").bit_length() - 1):
        partner = partner_2(mixed_part, "feat", bit_number)
        high_half = feat_index >> bit_number & 1 == 1
        mixed_part = jnp.where(high_half, partner - mixed_part, mixed_part + partner)
    rotated = lax.all_gather(
        (mixed_part * rotation_scale).astype(jnp.bfloat16), "feat", axis=1, tiled=True
    )
    in_limit = jnp.exp2(in_exponents.astype(jnp.float32))
    hidden_limit = jnp.exp2(hidden_exponents.astype(jnp.float32))
    gate_full, up_full, down_full = (
        lax.all_gather(gate_values, "tok", axis=1, tiled=True),
        lax.all_gather(up_values, "tok", axis=1, tiled=True),
        lax.all_gather(down_values, "tok", axis=1, tiled=True),
    )
    block_size = gate_values.shape[2]
    block_count = model_width // block_size
    hidden_local = hidden_exponents.shape[0]
    spike_in = jnp.clip(rotated.astype(jnp.float32), -in_limit, in_limit).astype(jnp.bfloat16)
    block_ids = jnp.arange(block_count, dtype=jnp.int32)
    gateup_place = (gateup_blocks[:, :, None] == block_ids[None, None, :]).astype(jnp.bfloat16)

    def dense(values):
        wide = jnp.einsum(
            "hkbc,hkn->nbhc", values, gateup_place, preferred_element_type=jnp.float32
        )
        return wide.astype(jnp.bfloat16).reshape(model_width, hidden_local)

    gate_sum = jnp.dot(spike_in, dense(gate_full), preferred_element_type=jnp.float32)
    upward = jnp.dot(spike_in, dense(up_full), preferred_element_type=jnp.float32)
    current = jax.nn.silu(gate_sum) * upward
    spiking_rate = jnp.clip(current, -hidden_limit, hidden_limit).astype(jnp.bfloat16)
    indicator = (
        down_blocks[:, :, None] == jnp.arange(block_count, dtype=jnp.int32)[None, None, :]
    ).astype(jnp.bfloat16)
    dense_down_weight = jnp.einsum(
        "hkbc,hkn->hbnc", down_full, indicator, preferred_element_type=jnp.float32
    ).astype(jnp.bfloat16)
    dense_down_weight = dense_down_weight.reshape(hidden_local, model_width)
    partial_block_value = jnp.dot(
        spiking_rate, dense_down_weight, preferred_element_type=jnp.float32
    )
    summed = lax.psum_scatter(partial_block_value, "feat", scatter_dimension=1, tiled=True)
    returned = lax.all_gather(summed.astype(jnp.bfloat16), "tok", axis=0, tiled=True)
    source_row = jnp.where(live_slot, start_of + position, 0)
    returned_rows = jnp.arange(returned.shape[0], dtype=jnp.int32)
    placer = (source_row[:, None] == returned_rows[None, :]) & live_slot[:, None]
    return jnp.dot(
        placer.astype(jnp.bfloat16), returned, preferred_element_type=jnp.float32
    ).astype(jnp.bfloat16)


def solution(mesh):
    in_specs = (
        P("tok", "feat"),
        P(),
        P(),
        P("feat"),
        P("feat", None),
        P("feat", None),
        P("feat", "tok", None, None),
        P("feat", "tok", None, None),
        P("feat", "tok", None, None),
    )
    out_specs = P("tok", "feat")
    same_groups = dict(mesh.shape) == {"tok": 2, "feat": 16}
    local = local_kernel if same_groups else local_general
    return jax.shard_map(local, mesh=mesh, in_specs=in_specs, out_specs=out_specs, check_vma=False)
```

```python
import math

import jax
import jax.numpy as jnp
from jax import lax
from jax.experimental import pallas as pl
from jax.experimental.pallas import tpu as pltpu
from jax.sharding import PartitionSpec as P

SEQS_DEV = 2
MESH_ID = pl.DeviceIdType.MESH
F32 = jnp.float32
BF16 = jnp.bfloat16


def slot_target(lengths, slots, seq_width):
    seq = slots // seq_width
    position = slots % seq_width
    start = jnp.zeros_like(slots)
    length = jnp.zeros_like(slots)
    running = 0
    for q, length_q in enumerate(lengths):
        here = seq == q
        start = jnp.where(here, running, start)
        length = jnp.where(here, length_q, length)
        running = running + length_q
    return jnp.where(position < length, start + position, -1)


def body(
    table_ref,
    tok_hbm,
    in_exp_hbm,
    hid_exp_hbm,
    gate_hbm,
    up_hbm,
    down_hbm,
    out_ref,
    tok_ref,
    in_exp_ref,
    hid_exp_ref,
    sign_ref,
    gate,
    up,
    down,
    peer_tok,
    all_tok,
    mixed,
    in_limit,
    spikes,
    snd_gu,
    rcv_gu,
    rate,
    snd_c,
    rcv_c,
    snd_x,
    rcv_x,
    acc,
    snd_y,
    rcv_y,
    snd_z,
    rcv_z,
    final,
    w_sem,
    raw_s,
    raw_r,
    agz_s,
    agz_r,
    agx_s,
    agx_r,
    agc_s,
    agc_r,
    gu_s,
    gu_r,
    rt_s,
    rt_r,
    c_s,
    c_r,
    x_s,
    x_r,
    y_s,
    y_r,
    z_s,
    z_r,
    fin_s,
    fin_r,
):
    t = lax.axis_index("tok")
    f = lax.axis_index("feat")
    z = f // 4
    x = (f // 2) % 2
    c = f % 2
    slots, width = tok_ref.shape
    live = slots
    half = live // 2
    side = slots // SEQS_DEV
    columns = rate.shape[0]
    mine = columns // 2
    kk = down.shape[1] - 1
    blocks = in_limit.shape[0]
    seq_at = blocks + kk

    dev_y = (1 - t, f)
    dev_c = (t, f + 1 - 2 * c)
    dev_x = (t, f + 2 - 4 * x)

    def z_at(d):
        return lax.rem(z + d, 4)

    def dev_z(d):
        return (t, z_at(d) * 4 + x * 2 + c)

    def chunk(zz, xx, cc):
        return zz * 4 + xx * 2 + cc

    def send(src, dst, ssem, rsem, dev):
        return pltpu.make_async_remote_copy(
            src_ref=src,
            dst_ref=dst,
            send_sem=ssem,
            recv_sem=rsem,
            device_id=dev,
            device_id_type=MESH_ID,
        )

    tok_copy = pltpu.make_async_copy(tok_hbm, tok_ref, w_sem.at[3])
    exp_copies = [
        pltpu.make_async_copy(in_exp_hbm, in_exp_ref, w_sem.at[4]),
        pltpu.make_async_copy(hid_exp_hbm, hid_exp_ref, w_sem.at[5]),
    ]
    tok_copy.start()
    for copy in exp_copies:
        copy.start()
    w_copies = [
        pltpu.make_async_copy(gate_hbm, gate, w_sem.at[0]),
        pltpu.make_async_copy(up_hbm, up, w_sem.at[1]),
        pltpu.make_async_copy(down_hbm, down.at[:, pl.ds(1, kk)], w_sem.at[2]),
    ]
    for copy in w_copies:
        copy.start()

    barrier = pltpu.get_barrier_semaphore()
    partners = [dev_y, dev_c, dev_x, dev_z(1), dev_z(2), dev_z(3)]
    for dev in partners:
        pl.semaphore_signal(barrier, inc=1, device_id=dev, device_id_type=MESH_ID)
    pl.semaphore_wait(barrier, len(partners))

    tok_copy.wait()

    raw = send(tok_ref, peer_tok, raw_s.at[0], raw_r.at[0], dev_y)
    raw.start()
    down[:, pl.ds(0, 1)] = jnp.zeros((columns, 1) + down.shape[2:], BF16)
    index = lax.broadcasted_iota(jnp.int32, (width, width), 0)
    parity = index & lax.broadcasted_iota(jnp.int32, (width, width), 1)
    shift = 1
    while shift < width.bit_length():
        parity = parity ^ (parity >> shift)
        shift *= 2
    sign_ref[...] = (1 - 2 * (parity & 1)).astype(F32).astype(BF16)
    for copy in exp_copies:
        copy.wait()
    in_limit[...] = jnp.exp2(in_exp_ref[...].astype(F32)).astype(BF16).astype(F32)
    lengths = [table_ref[0, seq_at + q] for q in range(table_ref.shape[1] - seq_at)]
    rows = lax.broadcasted_iota(jnp.int32, (live, slots), 0)
    lane_slots = lax.broadcasted_iota(jnp.int32, (live, slots), 1)

    def pick(group):
        target = slot_target(lengths, lane_slots + group * slots, side)
        return jnp.where(target == rows, 1.0, 0.0).astype(BF16)

    own_rows = jnp.dot(pick(t), tok_ref[...], preferred_element_type=F32)
    other_pick = pick(1 - t)
    raw.wait_recv()
    other_rows = jnp.dot(other_pick, peer_tok[...], preferred_element_type=F32)
    all_tok[f] = (own_rows + other_rows).astype(BF16)

    sent = [raw]

    def start(copy):
        copy.start()
        sent.append(copy)
        return copy

    def rotate_low(g):
        mixed[g] = jnp.dot(all_tok[g], sign_ref[...], preferred_element_type=F32)

    def forward_x(d, g):
        return start(send(all_tok.at[g], all_tok.at[g], agx_s.at[d], agx_r.at[d], dev_x))

    def forward_c(d, g):
        return start(send(all_tok.at[g], all_tok.at[g], agc_s.at[d], agc_r.at[d], dev_c))

    z_copies = [
        start(send(all_tok.at[f], all_tok.at[f], agz_s.at[d - 1], agz_r.at[d - 1], dev_z(d)))
        for d in (1, 2, 3)
    ]
    x_copies = [forward_x(0, f)]
    c_copies = [forward_c(0, f)]
    rotate_low(f)
    for d in (1, 3, 2):
        z_copies[d - 1].wait_recv()
        g = chunk(z_at(4 - d), x, c)
        x_copies.append(forward_x(d, g))
        c_copies.append(forward_c(d, g))
        rotate_low(g)
    for i, d in enumerate((0, 1, 3, 2)):
        x_copies[i].wait_recv()
        g = chunk(z_at(4 - d), 1 - x, c)
        c_copies.append(forward_c(4 + d, g))
        rotate_low(g)
    for i, d in enumerate((0, 1, 3, 2)):
        c_copies[i].wait_recv()
        rotate_low(chunk(z_at(4 - d), x, 1 - c))
    for i, d in enumerate((0, 1, 3, 2)):
        c_copies[4 + i].wait_recv()
        rotate_low(chunk(z_at(4 - d), 1 - x, 1 - c))

    chunks = mixed.shape[0]
    scale = 1.0 / math.sqrt(chunks * width)
    parts = width // 128

    def rotate_high(r, carry):
        at = pl.ds(pl.multiple_of(r * 16, 16), 16)
        for h in range(parts):
            vals = [mixed[i, at, pl.ds(h * 128, 128)] for i in range(chunks)]
            bit = 1
            while bit < chunks:
                nxt = list(vals)
                for i in range(chunks):
                    if not i & bit:
                        nxt[i] = vals[i] + vals[i | bit]
                        nxt[i | bit] = vals[i] - vals[i | bit]
                vals = nxt
                bit *= 2
            for i in range(chunks):
                n = parts * i + h
                limit = in_limit[pl.ds(n, 1), :]
                rotated = (vals[i] * scale).astype(BF16).astype(F32)
                spikes[n, at, :] = jnp.minimum(jnp.maximum(rotated, -limit), limit).astype(BF16)
        return carry

    lax.fori_loop(0, live // 16, rotate_high, 0)

    w_copies[0].wait()
    w_copies[1].wait()

    def pair_sums(j):
        lhs = jnp.concatenate([spikes[table_ref[j, blocks + k]] for k in range(kk)], axis=1)
        rhs = jnp.concatenate([gate[j], up[j]], axis=1)
        return jnp.dot(lhs, rhs, preferred_element_type=F32)

    def gu_copy(i):
        return send(snd_gu.at[i], rcv_gu.at[i], gu_s.at[i], gu_r.at[i], dev_y)

    def rate_copy(i):
        j = t * mine + i
        return send(rate.at[j], rate.at[j], rt_s.at[i], rt_r.at[i], dev_y)

    def give(i, carry):
        snd_gu[i] = pair_sums((1 - t) * mine + i).astype(BF16)
        gu_copy(i).start()
        return carry

    def take(i, carry):
        j = t * mine + i
        own = pair_sums(j)
        gu_copy(i).wait_recv()
        total = own + rcv_gu[i].astype(F32)
        gate_sum = total[:, :128]
        current = gate_sum / (1.0 + jnp.exp(-gate_sum)) * total[:, 128:]
        limit = jnp.exp2(hid_exp_ref[pl.ds(j, 1), :].astype(F32)).astype(BF16).astype(F32)
        rate[j] = jnp.minimum(jnp.maximum(current, -limit), limit).astype(BF16)
        rate_copy(i).start()
        return carry

    lax.fori_loop(0, mine, give, 0)
    lax.fori_loop(0, mine, take, 0)
    w_copies[2].wait()
    for i in range(mine):
        rate_copy(i).wait_recv()

    def down_chunk(g):
        lhs = jnp.concatenate([rate[j] for j in range(columns)], axis=1)
        cols = []
        for h in range(parts):
            n = g * parts + h
            cols.append(
                jnp.concatenate([down[j, table_ref[j, n]] for j in range(columns)], axis=0)
            )
        return jnp.dot(lhs, jnp.concatenate(cols, axis=1), preferred_element_type=F32)

    def z_turn(i):
        return z_at(jnp.where(i < 2, 2 + i, 3 - i))

    def core_copy(i):
        return send(snd_c.at[i], rcv_c.at[i], c_s.at[i], c_r.at[i], dev_c)

    def x_copy(i):
        return send(snd_x.at[i], rcv_x.at[i], x_s.at[i], x_r.at[i], dev_x)

    def y_copy(i):
        return send(snd_y.at[i], rcv_y.at[i], y_s.at[i], y_r.at[i], dev_y)

    def give_core_far(i, carry):
        snd_c[i] = down_chunk(chunk(z_turn(i), 1 - x, 1 - c)).astype(BF16)
        core_copy(i).start()
        return carry

    def give_core_near(i, carry):
        snd_c[4 + i] = down_chunk(chunk(z_turn(i), x, 1 - c)).astype(BF16)
        core_copy(4 + i).start()
        return carry

    def give_x(i, carry):
        own = down_chunk(chunk(z_turn(i), 1 - x, c))
        core_copy(i).wait_recv()
        snd_x[i] = (own + rcv_c[i].astype(F32)).astype(BF16)
        x_copy(i).start()
        return carry

    def keep(i, carry):
        own = down_chunk(chunk(z_turn(i), x, c))
        core_copy(4 + i).wait_recv()
        acc[i] = own + rcv_c[4 + i].astype(F32)
        return carry

    my_rows = pl.ds(pl.multiple_of(t * half, half), half)
    peer_rows = pl.ds(pl.multiple_of((1 - t) * half, half), half)

    def give_y(i, carry):
        x_copy(i).wait_recv()
        snd_y[i] = (acc[i, peer_rows, :] + rcv_x[i, peer_rows, :].astype(F32)).astype(BF16)
        y_copy(i).start()
        return carry

    lax.fori_loop(0, 4, give_core_far, 0)
    lax.fori_loop(0, 4, give_x, 0)
    lax.fori_loop(0, 4, give_core_near, 0)
    lax.fori_loop(0, 4, keep, 0)
    lax.fori_loop(0, 4, give_y, 0)

    def own_sum(i):
        y_copy(i).wait_recv()
        return (
            acc[i, my_rows, :] + rcv_x[i, my_rows, :].astype(F32) + rcv_y[i].astype(F32)
        )

    zs = []
    for i, d in enumerate((2, 3, 1)):
        snd_z[d - 1] = own_sum(i).astype(BF16)
        zs.append(
            start(send(snd_z.at[d - 1], rcv_z.at[d - 1], z_s.at[d - 1], z_r.at[d - 1], dev_z(d)))
        )
    total = own_sum(3)
    for copy, d in zip(zs, (2, 3, 1)):
        copy.wait_recv()
        total = total + rcv_z[d - 1].astype(F32)
    final[my_rows, :] = total.astype(BF16)
    fin = start(send(final.at[my_rows], final.at[my_rows], fin_s.at[0], fin_r.at[0], dev_y))
    slot_rows = lax.broadcasted_iota(jnp.int32, (slots, live), 0) + t * slots
    live_lanes = lax.broadcasted_iota(jnp.int32, (slots, live), 1)
    place = jnp.where(slot_target(lengths, slot_rows, side) == live_lanes, 1.0, 0.0).astype(BF16)
    fin.wait_recv()
    out_ref[...] = jnp.dot(place, final[...], preferred_element_type=F32).astype(BF16)

    for copy in sent:
        copy.wait_send()
    for i in range(mine):
        gu_copy(i).wait_send()
        rate_copy(i).wait_send()
    for i in range(8):
        core_copy(i).wait_send()
    for i in range(4):
        x_copy(i).wait_send()
        y_copy(i).wait_send()


def local_kernel(
    tokens,
    seq_lengths,
    in_exponents,
    hidden_exponents,
    gateup_blocks,
    down_blocks,
    gate_values,
    up_values,
    down_values,
):
    slots, width = tokens.shape
    columns, kk, side, _ = gate_values.shape
    model_width = in_exponents.shape[0]
    blocks = model_width // side
    chunks = model_width // width
    mine = columns // 2
    half = slots // 2
    t = lax.axis_index("tok")
    held = lax.dynamic_slice_in_dim(down_blocks, t * kk, kk, axis=1)
    match = held[:, :, None] == jnp.arange(blocks, dtype=jnp.int32)[None, None, :]
    number = jnp.arange(1, kk + 1, dtype=jnp.int32)[None, :, None]
    slot_of = jnp.sum(jnp.where(match, number, 0), axis=1)

    seq_count = seq_lengths.shape[0]
    table = jnp.concatenate(
        [
            slot_of,
            lax.dynamic_slice_in_dim(gateup_blocks, t * kk, kk, axis=1),
            jnp.broadcast_to(seq_lengths[None, :], (columns, seq_count)),
        ],
        axis=1,
    )

    vmem = pl.BlockSpec(memory_space=pltpu.VMEM)
    smem = pl.BlockSpec(memory_space=pltpu.SMEM)
    anywhere = pl.BlockSpec(memory_space=pl.ANY)
    dma = lambda n: pltpu.SemaphoreType.DMA((n,))
    buf = lambda *shape: pltpu.VMEM(shape, BF16)
    return pl.pallas_call(
        body,
        out_shape=jax.ShapeDtypeStruct((slots, width), BF16),
        in_specs=[smem] + [anywhere] * 6,
        out_specs=vmem,
        scratch_shapes=[
            buf(slots, width),
            pltpu.VMEM((blocks, side), jnp.int32),
            pltpu.VMEM((columns, side), jnp.int32),
            buf(width, width),
            buf(columns, kk * side, side),
            buf(columns, kk * side, side),
            buf(columns, kk + 1, side, side),
            buf(slots, width),
            buf(chunks, slots, width),
            pltpu.VMEM((chunks, slots, width), F32),
            pltpu.VMEM((blocks, side), F32),
            buf(blocks, slots, side),
            buf(mine, slots, 2 * side),
            buf(mine, slots, 2 * side),
            buf(columns, slots, side),
            buf(8, slots, width),
            buf(8, slots, width),
            buf(4, slots, width),
            buf(4, slots, width),
            pltpu.VMEM((4, slots, width), F32),
            buf(4, half, width),
            buf(4, half, width),
            buf(3, half, width),
            buf(3, half, width),
            buf(slots, width),
            dma(6),
            dma(1),
            dma(1),
            dma(3),
            dma(3),
            dma(4),
            dma(4),
            dma(8),
            dma(8),
            dma(mine),
            dma(mine),
            dma(mine),
            dma(mine),
            dma(8),
            dma(8),
            dma(4),
            dma(4),
            dma(4),
            dma(4),
            dma(3),
            dma(3),
            dma(1),
            dma(1),
        ],
        compiler_params=pltpu.CompilerParams(
            collective_id=0, has_side_effects=True, vmem_limit_bytes=60 * 1024 * 1024
        ),
        name="spiking_ffn",
    )(
        table,
        tokens,
        in_exponents.reshape(blocks, side),
        hidden_exponents.reshape(columns, side),
        gate_values.reshape(columns, kk * side, side),
        up_values.reshape(columns, kk * side, side),
        down_values,
    )


def partner_2(value, axis, stride):
    mask = 2**stride
    pairs = [(source, source ^ mask) for source in range(lax.axis_size(axis))]
    return lax.ppermute(value, axis, pairs)


def sign_table(order_size, value_type):
    indices = jnp.arange(order_size, dtype=jnp.int32)
    shared = indices[:, None] & indices[None, :]
    parity = jnp.zeros((order_size, order_size), jnp.int32)
    for bit_number in range(max(1, (order_size - 1).bit_length())):
        parity = parity ^ shared >> bit_number & 1
    return (1 - 2 * parity).astype(value_type)


def local_general(
    tokens,
    seq_lengths,
    in_exponents,
    hidden_exponents,
    gateup_blocks,
    down_blocks,
    gate_values,
    up_values,
    down_values,
):
    slot_count, feat_local = tokens.shape
    model_width = in_exponents.shape[0]
    seq_width = slot_count // SEQS_DEV
    tok_index = lax.axis_index("tok")
    seq_count = seq_lengths.shape[0]
    earlier = jnp.tril(jnp.ones((seq_count, seq_count), jnp.int32))
    seq_ends = jnp.sum(earlier * seq_lengths[None, :], axis=1)
    seq_starts = seq_ends - seq_lengths
    seq_ids = jnp.arange(seq_lengths.shape[0], dtype=jnp.int32)
    slot_ids = jnp.arange(slot_count, dtype=jnp.int32)
    seq_of = tok_index * SEQS_DEV + slot_ids // seq_width
    position = slot_ids % seq_width
    same_seq = seq_of[:, None] == seq_ids[None, :]
    length_of = jnp.sum(jnp.where(same_seq, seq_lengths[None, :], 0), axis=1)
    start_of = jnp.sum(jnp.where(same_seq, seq_starts[None, :], 0), axis=1)
    live_slot = position < length_of
    pooled = lax.all_gather(tokens, "tok", axis=0, tiled=True)
    wanted = tok_index * seq_width + jnp.arange(seq_width, dtype=jnp.int32)
    owner_seq = jnp.sum((seq_ends[None, :] <= wanted[:, None]).astype(jnp.int32), axis=1)
    owner_match = owner_seq[:, None] == seq_ids[None, :]
    offset = wanted - jnp.sum(jnp.where(owner_match, seq_starts[None, :], 0), axis=1)
    picked_slot = owner_seq * seq_width + offset
    pooled_slots = jnp.arange(pooled.shape[0], dtype=jnp.int32)
    picker = (picked_slot[:, None] == pooled_slots[None, :]).astype(jnp.bfloat16)
    picked = jnp.dot(picker, pooled, preferred_element_type=jnp.float32).astype(jnp.bfloat16)
    row_count = picked.shape[0]
    rotation_scale = 1.0 / math.sqrt(model_width)
    mixed_part = jnp.dot(
        picked, sign_table(feat_local, jnp.bfloat16), preferred_element_type=jnp.float32
    )
    feat_index = lax.axis_index("feat")
    for bit_number in range(lax.axis_size("feat").bit_length() - 1):
        partner = partner_2(mixed_part, "feat", bit_number)
        high_half = feat_index >> bit_number & 1 == 1
        mixed_part = jnp.where(high_half, partner - mixed_part, mixed_part + partner)
    rotated = lax.all_gather(
        (mixed_part * rotation_scale).astype(jnp.bfloat16), "feat", axis=1, tiled=True
    )
    in_limit = jnp.exp2(in_exponents.astype(jnp.float32))
    hidden_limit = jnp.exp2(hidden_exponents.astype(jnp.float32))
    gate_full, up_full, down_full = (
        lax.all_gather(gate_values, "tok", axis=1, tiled=True),
        lax.all_gather(up_values, "tok", axis=1, tiled=True),
        lax.all_gather(down_values, "tok", axis=1, tiled=True),
    )
    block_size = gate_values.shape[2]
    block_count = model_width // block_size
    hidden_local = hidden_exponents.shape[0]
    spike_in = jnp.clip(rotated.astype(jnp.float32), -in_limit, in_limit).astype(jnp.bfloat16)
    block_ids = jnp.arange(block_count, dtype=jnp.int32)
    gateup_place = (gateup_blocks[:, :, None] == block_ids[None, None, :]).astype(jnp.bfloat16)

    def dense(values):
        wide = jnp.einsum(
            "hkbc,hkn->nbhc", values, gateup_place, preferred_element_type=jnp.float32
        )
        return wide.astype(jnp.bfloat16).reshape(model_width, hidden_local)

    gate_sum = jnp.dot(spike_in, dense(gate_full), preferred_element_type=jnp.float32)
    upward = jnp.dot(spike_in, dense(up_full), preferred_element_type=jnp.float32)
    current = jax.nn.silu(gate_sum) * upward
    spiking_rate = jnp.clip(current, -hidden_limit, hidden_limit).astype(jnp.bfloat16)
    indicator = (
        down_blocks[:, :, None] == jnp.arange(block_count, dtype=jnp.int32)[None, None, :]
    ).astype(jnp.bfloat16)
    dense_down_weight = jnp.einsum(
        "hkbc,hkn->hbnc", down_full, indicator, preferred_element_type=jnp.float32
    ).astype(jnp.bfloat16)
    dense_down_weight = dense_down_weight.reshape(hidden_local, model_width)
    partial_block_value = jnp.dot(
        spiking_rate, dense_down_weight, preferred_element_type=jnp.float32
    )
    summed = lax.psum_scatter(partial_block_value, "feat", scatter_dimension=1, tiled=True)
    returned = lax.all_gather(summed.astype(jnp.bfloat16), "tok", axis=0, tiled=True)
    source_row = jnp.where(live_slot, start_of + position, 0)
    returned_rows = jnp.arange(returned.shape[0], dtype=jnp.int32)
    placer = (source_row[:, None] == returned_rows[None, :]) & live_slot[:, None]
    return jnp.dot(
        placer.astype(jnp.bfloat16), returned, preferred_element_type=jnp.float32
    ).astype(jnp.bfloat16)


def solution(mesh):
    in_specs = (
        P("tok", "feat"),
        P(),
        P(),
        P("feat"),
        P("feat", None),
        P("feat", None),
        P("feat", "tok", None, None),
        P("feat", "tok", None, None),
        P("feat", "tok", None, None),
    )
    out_specs = P("tok", "feat")
    same_groups = dict(mesh.shape) == {"tok": 2, "feat": 16}
    local = local_kernel if same_groups else local_general
    return jax.shard_map(local, mesh=mesh, in_specs=in_specs, out_specs=out_specs, check_vma=False)
```

```python
import math

import jax
import jax.numpy as jnp
from jax import lax
from jax.experimental import pallas as pl
from jax.experimental.pallas import tpu as pltpu
from jax.sharding import PartitionSpec as P

SEQS_DEV = 2
MESH_ID = pl.DeviceIdType.MESH
F32 = jnp.float32
BF16 = jnp.bfloat16


def slot_target(lengths, slots, seq_width):
    seq = slots // seq_width
    position = slots % seq_width
    start = jnp.zeros_like(slots)
    length = jnp.zeros_like(slots)
    running = 0
    for q, length_q in enumerate(lengths):
        here = seq == q
        start = jnp.where(here, running, start)
        length = jnp.where(here, length_q, length)
        running = running + length_q
    return jnp.where(position < length, start + position, -1)


def body(
    lengths_hbm,
    gateup_hbm,
    held_hbm,
    tok_hbm,
    in_exp_hbm,
    hid_exp_hbm,
    gate_hbm,
    up_hbm,
    down_hbm,
    out_ref,
    lengths_ref,
    gateup_ref,
    held_ref,
    slot_vec,
    slot_of_ref,
    tok_ref,
    in_exp_ref,
    hid_exp_ref,
    sign_ref,
    gate,
    up,
    down,
    peer_tok,
    all_tok,
    mixed,
    in_limit,
    spikes,
    snd_gu,
    rcv_gu,
    rate,
    snd_c,
    rcv_c,
    snd_x,
    rcv_x,
    acc,
    snd_y,
    rcv_y,
    snd_z,
    rcv_z,
    w_sem,
    raw_s,
    raw_r,
    agz_s,
    agz_r,
    agx_s,
    agx_r,
    agc_s,
    agc_r,
    gu_s,
    gu_r,
    rt_s,
    rt_r,
    c_s,
    c_r,
    x_s,
    x_r,
    y_s,
    y_r,
    z_s,
    z_r,
):
    t = lax.axis_index("tok")
    f = lax.axis_index("feat")
    z = f // 4
    x = (f // 2) % 2
    c = f % 2
    slots, width = tok_ref.shape
    live = slots
    side = slots // SEQS_DEV
    columns = rate.shape[0]
    mine = columns // 2
    kk = down.shape[1] - 1

    dev_y = (1 - t, f)
    dev_c = (t, f + 1 - 2 * c)
    dev_x = (t, f + 2 - 4 * x)

    def z_at(d):
        return lax.rem(z + d, 4)

    def dev_z(d):
        return (t, z_at(d) * 4 + x * 2 + c)

    def chunk(zz, xx, cc):
        return zz * 4 + xx * 2 + cc

    def send(src, dst, ssem, rsem, dev):
        return pltpu.make_async_remote_copy(
            src_ref=src,
            dst_ref=dst,
            send_sem=ssem,
            recv_sem=rsem,
            device_id=dev,
            device_id_type=MESH_ID,
        )

    tok_copy = pltpu.make_async_copy(tok_hbm, tok_ref, w_sem.at[3])
    exp_copies = [
        pltpu.make_async_copy(in_exp_hbm, in_exp_ref, w_sem.at[4]),
        pltpu.make_async_copy(hid_exp_hbm, hid_exp_ref, w_sem.at[5]),
        pltpu.make_async_copy(lengths_hbm, lengths_ref, w_sem.at[6]),
        pltpu.make_async_copy(gateup_hbm, gateup_ref, w_sem.at[7]),
        pltpu.make_async_copy(held_hbm, held_ref, w_sem.at[8]),
    ]
    tok_copy.start()
    for copy in exp_copies:
        copy.start()
    w_copies = [
        pltpu.make_async_copy(gate_hbm, gate, w_sem.at[0]),
        pltpu.make_async_copy(up_hbm, up, w_sem.at[1]),
        pltpu.make_async_copy(down_hbm, down.at[:, pl.ds(1, kk)], w_sem.at[2]),
    ]
    for copy in w_copies:
        copy.start()

    barrier = pltpu.get_barrier_semaphore()
    partners = [dev_y, dev_c, dev_x, dev_z(1), dev_z(2), dev_z(3)]
    for dev in partners:
        pl.semaphore_signal(barrier, inc=1, device_id=dev, device_id_type=MESH_ID)
    pl.semaphore_wait(barrier, len(partners))

    tok_copy.wait()

    raw = send(tok_ref, peer_tok, raw_s.at[0], raw_r.at[0], dev_y)
    raw.start()
    down[:, pl.ds(0, 1)] = jnp.zeros((columns, 1) + down.shape[2:], BF16)
    index = lax.broadcasted_iota(jnp.int32, (width, width), 0)
    parity = index & lax.broadcasted_iota(jnp.int32, (width, width), 1)
    shift = 1
    while shift < width.bit_length():
        parity = parity ^ (parity >> shift)
        shift *= 2
    sign_ref[...] = (1 - 2 * (parity & 1)).astype(F32).astype(BF16)
    for copy in exp_copies:
        copy.wait()
    held = jnp.where(t == 0, held_ref[:, :kk], held_ref[:, kk:])
    block_ids = lax.broadcasted_iota(jnp.int32, slot_vec.shape, 1)
    slot_of = jnp.zeros(slot_vec.shape, jnp.int32)
    for k in range(kk):
        slot_of = jnp.where(held[:, k : k + 1] == block_ids, k + 1, slot_of)
    slot_vec[...] = slot_of
    slot_copy = pltpu.make_async_copy(slot_vec, slot_of_ref, w_sem.at[9])
    slot_copy.start()
    in_limit[...] = jnp.exp2(in_exp_ref[...].astype(F32)).astype(BF16).astype(F32)
    lengths = [lengths_ref[q] for q in range(lengths_ref.shape[0])]
    rows = lax.broadcasted_iota(jnp.int32, (live, slots), 0)
    lane_slots = lax.broadcasted_iota(jnp.int32, (live, slots), 1)

    def pick(group):
        target = slot_target(lengths, lane_slots + group * slots, side)
        return jnp.where(target == rows, 1.0, 0.0).astype(BF16)

    own_rows = jnp.dot(pick(t), tok_ref[...], preferred_element_type=F32)
    other_pick = pick(1 - t)
    raw.wait_recv()
    other_rows = jnp.dot(other_pick, peer_tok[...], preferred_element_type=F32)
    all_tok[f] = (own_rows + other_rows).astype(BF16)

    sent = [raw]

    def start(copy):
        copy.start()
        sent.append(copy)
        return copy

    def rotate_low(g):
        mixed[g] = jnp.dot(all_tok[g], sign_ref[...], preferred_element_type=F32)

    def forward_x(d, g):
        return start(send(all_tok.at[g], all_tok.at[g], agx_s.at[d], agx_r.at[d], dev_x))

    def forward_c(d, g):
        return start(send(all_tok.at[g], all_tok.at[g], agc_s.at[d], agc_r.at[d], dev_c))

    z_copies = [
        start(send(all_tok.at[f], all_tok.at[f], agz_s.at[d - 1], agz_r.at[d - 1], dev_z(d)))
        for d in (1, 2, 3)
    ]
    x_copies = [forward_x(0, f)]
    c_copies = [forward_c(0, f)]
    rotate_low(f)
    for d in (1, 3, 2):
        z_copies[d - 1].wait_recv()
        g = chunk(z_at(4 - d), x, c)
        x_copies.append(forward_x(d, g))
        c_copies.append(forward_c(d, g))
        rotate_low(g)
    for i, d in enumerate((0, 1, 3, 2)):
        x_copies[i].wait_recv()
        g = chunk(z_at(4 - d), 1 - x, c)
        c_copies.append(forward_c(4 + d, g))
        rotate_low(g)
    for i, d in enumerate((0, 1, 3, 2)):
        c_copies[i].wait_recv()
        rotate_low(chunk(z_at(4 - d), x, 1 - c))
    for i, d in enumerate((0, 1, 3, 2)):
        c_copies[4 + i].wait_recv()
        rotate_low(chunk(z_at(4 - d), 1 - x, 1 - c))

    chunks = mixed.shape[0]
    scale = 1.0 / math.sqrt(chunks * width)
    parts = width // 128

    def rotate_high(r, carry):
        at = pl.ds(pl.multiple_of(r * 16, 16), 16)
        for h in range(parts):
            vals = [mixed[i, at, pl.ds(h * 128, 128)] for i in range(chunks)]
            bit = 1
            while bit < chunks:
                nxt = list(vals)
                for i in range(chunks):
                    if not i & bit:
                        nxt[i] = vals[i] + vals[i | bit]
                        nxt[i | bit] = vals[i] - vals[i | bit]
                vals = nxt
                bit *= 2
            for i in range(chunks):
                n = parts * i + h
                limit = in_limit[pl.ds(n, 1), :]
                rotated = (vals[i] * scale).astype(BF16).astype(F32)
                spikes[n, at, :] = jnp.minimum(jnp.maximum(rotated, -limit), limit).astype(BF16)
        return carry

    lax.fori_loop(0, live // 16, rotate_high, 0)

    w_copies[0].wait()
    w_copies[1].wait()

    def pair_sums(j):
        lhs = jnp.concatenate([spikes[gateup_ref[j, t * kk + k]] for k in range(kk)], axis=1)
        rhs = jnp.concatenate([gate[j], up[j]], axis=1)
        return jnp.dot(lhs, rhs, preferred_element_type=F32)

    def gu_copy(i):
        return send(snd_gu.at[i], rcv_gu.at[i], gu_s.at[i], gu_r.at[i], dev_y)

    def rate_copy(i):
        j = t * mine + i
        return send(rate.at[j], rate.at[j], rt_s.at[i], rt_r.at[i], dev_y)

    def give(i, carry):
        snd_gu[i] = pair_sums((1 - t) * mine + i).astype(BF16)
        gu_copy(i).start()
        return carry

    def take(i, carry):
        j = t * mine + i
        own = pair_sums(j)
        gu_copy(i).wait_recv()
        total = own + rcv_gu[i].astype(F32)
        gate_sum = total[:, :128]
        current = gate_sum / (1.0 + jnp.exp(-gate_sum)) * total[:, 128:]
        limit = jnp.exp2(hid_exp_ref[pl.ds(j, 1), :].astype(F32)).astype(BF16).astype(F32)
        rate[j] = jnp.minimum(jnp.maximum(current, -limit), limit).astype(BF16)
        rate_copy(i).start()
        return carry

    lax.fori_loop(0, mine, give, 0)
    lax.fori_loop(0, mine, take, 0)
    w_copies[2].wait()
    slot_copy.wait()
    for i in range(mine):
        rate_copy(i).wait_recv()

    def down_chunk(g):
        lhs = jnp.concatenate([rate[j] for j in range(columns)], axis=1)
        cols = []
        for h in range(parts):
            n = g * parts + h
            cols.append(
                jnp.concatenate([down[j, slot_of_ref[j, n]] for j in range(columns)], axis=0)
            )
        return jnp.dot(lhs, jnp.concatenate(cols, axis=1), preferred_element_type=F32)

    def z_turn(i):
        return z_at(jnp.where(i < 2, 2 + i, 3 - i))

    def core_copy(i):
        return send(snd_c.at[i], rcv_c.at[i], c_s.at[i], c_r.at[i], dev_c)

    def x_copy(i):
        return send(snd_x.at[i], rcv_x.at[i], x_s.at[i], x_r.at[i], dev_x)

    def give_core_far(i, carry):
        snd_c[i] = down_chunk(chunk(z_turn(i), 1 - x, 1 - c)).astype(BF16)
        core_copy(i).start()
        return carry

    def give_core_near(i, carry):
        snd_c[4 + i] = down_chunk(chunk(z_turn(i), x, 1 - c)).astype(BF16)
        core_copy(4 + i).start()
        return carry

    def give_x(i, carry):
        own = down_chunk(chunk(z_turn(i), 1 - x, c))
        core_copy(i).wait_recv()
        snd_x[i] = (own + rcv_c[i].astype(F32)).astype(BF16)
        x_copy(i).start()
        return carry

    def keep(i, carry):
        own = down_chunk(chunk(z_turn(i), x, c))
        core_copy(4 + i).wait_recv()
        acc[i] = own + rcv_c[4 + i].astype(F32)
        return carry

    lax.fori_loop(0, 4, give_core_far, 0)
    lax.fori_loop(0, 4, give_x, 0)
    lax.fori_loop(0, 4, give_core_near, 0)
    lax.fori_loop(0, 4, keep, 0)

    def own_sum(i):
        x_copy(i).wait_recv()
        return acc[i] + rcv_x[i].astype(F32)

    zs = []
    for i, d in enumerate((2, 3, 1)):
        snd_z[d - 1] = own_sum(i).astype(BF16)
        zs.append(
            start(send(snd_z.at[d - 1], rcv_z.at[d - 1], z_s.at[d - 1], z_r.at[d - 1], dev_z(d)))
        )
    total = own_sum(3)
    for copy, d in zip(zs, (2, 3, 1)):
        copy.wait_recv()
        total = total + rcv_z[d - 1].astype(F32)
    snd_y[...] = total.astype(BF16)
    fin = start(send(snd_y, rcv_y, y_s.at[0], y_r.at[0], dev_y))
    slot_rows = lax.broadcasted_iota(jnp.int32, (slots, live), 0) + t * slots
    live_lanes = lax.broadcasted_iota(jnp.int32, (slots, live), 1)
    place = jnp.where(slot_target(lengths, slot_rows, side) == live_lanes, 1.0, 0.0).astype(BF16)
    fin.wait_recv()
    result = (total + rcv_y[...].astype(F32)).astype(BF16)
    out_ref[...] = jnp.dot(place, result, preferred_element_type=F32).astype(BF16)

    for copy in sent:
        copy.wait_send()
    for i in range(mine):
        gu_copy(i).wait_send()
        rate_copy(i).wait_send()
    for i in range(8):
        core_copy(i).wait_send()
    for i in range(4):
        x_copy(i).wait_send()


def local_kernel(
    tokens,
    seq_lengths,
    in_exponents,
    hidden_exponents,
    gateup_blocks,
    down_blocks,
    gate_values,
    up_values,
    down_values,
):
    slots, width = tokens.shape
    columns, kk, side, _ = gate_values.shape
    model_width = in_exponents.shape[0]
    blocks = model_width // side
    chunks = model_width // width
    mine = columns // 2
    t = lax.axis_index("tok")
    vmem = pl.BlockSpec(memory_space=pltpu.VMEM)
    anywhere = pl.BlockSpec(memory_space=pl.ANY)
    dma = lambda n: pltpu.SemaphoreType.DMA((n,))
    buf = lambda *shape: pltpu.VMEM(shape, BF16)
    return pl.pallas_call(
        body,
        out_shape=jax.ShapeDtypeStruct((slots, width), BF16),
        in_specs=[anywhere] * 9,
        out_specs=vmem,
        scratch_shapes=[
            pltpu.SMEM(seq_lengths.shape, jnp.int32),
            pltpu.SMEM(gateup_blocks.shape, jnp.int32),
            pltpu.VMEM(down_blocks.shape, jnp.int32),
            pltpu.VMEM((columns, 128), jnp.int32),
            pltpu.SMEM((columns, 128), jnp.int32),
            buf(slots, width),
            pltpu.VMEM((blocks, side), jnp.int32),
            pltpu.VMEM((columns, side), jnp.int32),
            buf(width, width),
            buf(columns, kk * side, side),
            buf(columns, kk * side, side),
            buf(columns, kk + 1, side, side),
            buf(slots, width),
            buf(chunks, slots, width),
            pltpu.VMEM((chunks, slots, width), F32),
            pltpu.VMEM((blocks, side), F32),
            buf(blocks, slots, side),
            buf(mine, slots, 2 * side),
            buf(mine, slots, 2 * side),
            buf(columns, slots, side),
            buf(8, slots, width),
            buf(8, slots, width),
            buf(4, slots, width),
            buf(4, slots, width),
            pltpu.VMEM((4, slots, width), F32),
            buf(slots, width),
            buf(slots, width),
            buf(3, slots, width),
            buf(3, slots, width),
            dma(10),
            dma(1),
            dma(1),
            dma(3),
            dma(3),
            dma(4),
            dma(4),
            dma(8),
            dma(8),
            dma(mine),
            dma(mine),
            dma(mine),
            dma(mine),
            dma(8),
            dma(8),
            dma(4),
            dma(4),
            dma(1),
            dma(1),
            dma(3),
            dma(3),
        ],
        compiler_params=pltpu.CompilerParams(
            collective_id=0, has_side_effects=True, vmem_limit_bytes=60 * 1024 * 1024
        ),
        name="spiking_ffn",
    )(
        seq_lengths,
        gateup_blocks,
        down_blocks,
        tokens,
        in_exponents.reshape(blocks, side),
        hidden_exponents.reshape(columns, side),
        gate_values.reshape(columns, kk * side, side),
        up_values.reshape(columns, kk * side, side),
        down_values,
    )


def partner_2(value, axis, stride):
    mask = 2**stride
    pairs = [(source, source ^ mask) for source in range(lax.axis_size(axis))]
    return lax.ppermute(value, axis, pairs)


def sign_table(order_size, value_type):
    indices = jnp.arange(order_size, dtype=jnp.int32)
    shared = indices[:, None] & indices[None, :]
    parity = jnp.zeros((order_size, order_size), jnp.int32)
    for bit_number in range(max(1, (order_size - 1).bit_length())):
        parity = parity ^ shared >> bit_number & 1
    return (1 - 2 * parity).astype(value_type)


def local_general(
    tokens,
    seq_lengths,
    in_exponents,
    hidden_exponents,
    gateup_blocks,
    down_blocks,
    gate_values,
    up_values,
    down_values,
):
    slot_count, feat_local = tokens.shape
    model_width = in_exponents.shape[0]
    seq_width = slot_count // SEQS_DEV
    tok_index = lax.axis_index("tok")
    seq_count = seq_lengths.shape[0]
    earlier = jnp.tril(jnp.ones((seq_count, seq_count), jnp.int32))
    seq_ends = jnp.sum(earlier * seq_lengths[None, :], axis=1)
    seq_starts = seq_ends - seq_lengths
    seq_ids = jnp.arange(seq_lengths.shape[0], dtype=jnp.int32)
    slot_ids = jnp.arange(slot_count, dtype=jnp.int32)
    seq_of = tok_index * SEQS_DEV + slot_ids // seq_width
    position = slot_ids % seq_width
    same_seq = seq_of[:, None] == seq_ids[None, :]
    length_of = jnp.sum(jnp.where(same_seq, seq_lengths[None, :], 0), axis=1)
    start_of = jnp.sum(jnp.where(same_seq, seq_starts[None, :], 0), axis=1)
    live_slot = position < length_of
    pooled = lax.all_gather(tokens, "tok", axis=0, tiled=True)
    wanted = tok_index * seq_width + jnp.arange(seq_width, dtype=jnp.int32)
    owner_seq = jnp.sum((seq_ends[None, :] <= wanted[:, None]).astype(jnp.int32), axis=1)
    owner_match = owner_seq[:, None] == seq_ids[None, :]
    offset = wanted - jnp.sum(jnp.where(owner_match, seq_starts[None, :], 0), axis=1)
    picked_slot = owner_seq * seq_width + offset
    pooled_slots = jnp.arange(pooled.shape[0], dtype=jnp.int32)
    picker = (picked_slot[:, None] == pooled_slots[None, :]).astype(jnp.bfloat16)
    picked = jnp.dot(picker, pooled, preferred_element_type=jnp.float32).astype(jnp.bfloat16)
    row_count = picked.shape[0]
    rotation_scale = 1.0 / math.sqrt(model_width)
    mixed_part = jnp.dot(
        picked, sign_table(feat_local, jnp.bfloat16), preferred_element_type=jnp.float32
    )
    feat_index = lax.axis_index("feat")
    for bit_number in range(lax.axis_size("feat").bit_length() - 1):
        partner = partner_2(mixed_part, "feat", bit_number)
        high_half = feat_index >> bit_number & 1 == 1
        mixed_part = jnp.where(high_half, partner - mixed_part, mixed_part + partner)
    rotated = lax.all_gather(
        (mixed_part * rotation_scale).astype(jnp.bfloat16), "feat", axis=1, tiled=True
    )
    in_limit = jnp.exp2(in_exponents.astype(jnp.float32))
    hidden_limit = jnp.exp2(hidden_exponents.astype(jnp.float32))
    gate_full, up_full, down_full = (
        lax.all_gather(gate_values, "tok", axis=1, tiled=True),
        lax.all_gather(up_values, "tok", axis=1, tiled=True),
        lax.all_gather(down_values, "tok", axis=1, tiled=True),
    )
    block_size = gate_values.shape[2]
    block_count = model_width // block_size
    hidden_local = hidden_exponents.shape[0]
    spike_in = jnp.clip(rotated.astype(jnp.float32), -in_limit, in_limit).astype(jnp.bfloat16)
    block_ids = jnp.arange(block_count, dtype=jnp.int32)
    gateup_place = (gateup_blocks[:, :, None] == block_ids[None, None, :]).astype(jnp.bfloat16)

    def dense(values):
        wide = jnp.einsum(
            "hkbc,hkn->nbhc", values, gateup_place, preferred_element_type=jnp.float32
        )
        return wide.astype(jnp.bfloat16).reshape(model_width, hidden_local)

    gate_sum = jnp.dot(spike_in, dense(gate_full), preferred_element_type=jnp.float32)
    upward = jnp.dot(spike_in, dense(up_full), preferred_element_type=jnp.float32)
    current = jax.nn.silu(gate_sum) * upward
    spiking_rate = jnp.clip(current, -hidden_limit, hidden_limit).astype(jnp.bfloat16)
    indicator = (
        down_blocks[:, :, None] == jnp.arange(block_count, dtype=jnp.int32)[None, None, :]
    ).astype(jnp.bfloat16)
    dense_down_weight = jnp.einsum(
        "hkbc,hkn->hbnc", down_full, indicator, preferred_element_type=jnp.float32
    ).astype(jnp.bfloat16)
    dense_down_weight = dense_down_weight.reshape(hidden_local, model_width)
    partial_block_value = jnp.dot(
        spiking_rate, dense_down_weight, preferred_element_type=jnp.float32
    )
    summed = lax.psum_scatter(partial_block_value, "feat", scatter_dimension=1, tiled=True)
    returned = lax.all_gather(summed.astype(jnp.bfloat16), "tok", axis=0, tiled=True)
    source_row = jnp.where(live_slot, start_of + position, 0)
    returned_rows = jnp.arange(returned.shape[0], dtype=jnp.int32)
    placer = (source_row[:, None] == returned_rows[None, :]) & live_slot[:, None]
    return jnp.dot(
        placer.astype(jnp.bfloat16), returned, preferred_element_type=jnp.float32
    ).astype(jnp.bfloat16)


def solution(mesh):
    in_specs = (
        P("tok", "feat"),
        P(),
        P(),
        P("feat"),
        P("feat", None),
        P("feat", None),
        P("feat", "tok", None, None),
        P("feat", "tok", None, None),
        P("feat", "tok", None, None),
    )
    out_specs = P("tok", "feat")
    same_groups = dict(mesh.shape) == {"tok": 2, "feat": 16}
    local = local_kernel if same_groups else local_general
    return jax.shard_map(local, mesh=mesh, in_specs=in_specs, out_specs=out_specs, check_vma=False)
```

```python
import math

import jax
import jax.numpy as jnp
from jax import lax
from jax.experimental import pallas as pl
from jax.experimental.pallas import tpu as pltpu
from jax.sharding import PartitionSpec as P

SEQS_DEV = 2
MESH_ID = pl.DeviceIdType.MESH
F32 = jnp.float32
BF16 = jnp.bfloat16


def slot_target(lengths, slots, seq_width):
    seq = slots // seq_width
    position = slots % seq_width
    start = jnp.zeros_like(slots)
    length = jnp.zeros_like(slots)
    running = 0
    for q, length_q in enumerate(lengths):
        here = seq == q
        start = jnp.where(here, running, start)
        length = jnp.where(here, length_q, length)
        running = running + length_q
    return jnp.where(position < length, start + position, -1)


def body(
    lengths_hbm,
    gateup_hbm,
    held_hbm,
    tok_hbm,
    in_exp_hbm,
    hid_exp_hbm,
    gate_hbm,
    up_hbm,
    down_hbm,
    out_ref,
    lengths_ref,
    gateup_ref,
    held_ref,
    slot_vec,
    slot_of_ref,
    tok_ref,
    in_exp_ref,
    hid_exp_ref,
    sign_ref,
    gate,
    up,
    down,
    peer_tok,
    all_tok,
    mixed,
    in_limit,
    spikes,
    snd_gu,
    rcv_gu,
    rate,
    snd_c,
    rcv_c,
    snd_x,
    rcv_x,
    acc,
    snd_y,
    rcv_y,
    snd_z,
    rcv_z,
    snd_yr,
    rcv_yr,
    snd_xr,
    rcv_xr,
    snd_zr,
    rcv_zr,
    final,
    w_sem,
    raw_s,
    raw_r,
    agz_s,
    agz_r,
    agx_s,
    agx_r,
    agc_s,
    agc_r,
    gu_s,
    gu_r,
    rt_s,
    rt_r,
    c_s,
    c_r,
    x_s,
    x_r,
    y_s,
    y_r,
    z_s,
    z_r,
    yr_s,
    yr_r,
    xr_s,
    xr_r,
):
    t = lax.axis_index("tok")
    f = lax.axis_index("feat")
    z = f // 4
    x = (f // 2) % 2
    c = f % 2
    slots, width = tok_ref.shape
    live = slots
    side = slots // SEQS_DEV
    columns = rate.shape[0]
    mine = columns // 2
    kk = down.shape[1] - 1

    dev_y = (1 - t, f)
    dev_c = (t, f + 1 - 2 * c)
    dev_x = (t, f + 2 - 4 * x)

    def z_at(d):
        return lax.rem(z + d, 4)

    def dev_z(d):
        return (t, z_at(d) * 4 + x * 2 + c)

    def chunk(zz, xx, cc):
        return zz * 4 + xx * 2 + cc

    def send(src, dst, ssem, rsem, dev):
        return pltpu.make_async_remote_copy(
            src_ref=src,
            dst_ref=dst,
            send_sem=ssem,
            recv_sem=rsem,
            device_id=dev,
            device_id_type=MESH_ID,
        )

    tok_copy = pltpu.make_async_copy(tok_hbm, tok_ref, w_sem.at[3])
    exp_copies = [
        pltpu.make_async_copy(in_exp_hbm, in_exp_ref, w_sem.at[4]),
        pltpu.make_async_copy(hid_exp_hbm, hid_exp_ref, w_sem.at[5]),
        pltpu.make_async_copy(lengths_hbm, lengths_ref, w_sem.at[6]),
        pltpu.make_async_copy(gateup_hbm, gateup_ref, w_sem.at[7]),
        pltpu.make_async_copy(held_hbm, held_ref, w_sem.at[8]),
    ]
    tok_copy.start()
    for copy in exp_copies:
        copy.start()
    w_copies = [
        pltpu.make_async_copy(gate_hbm, gate, w_sem.at[0]),
        pltpu.make_async_copy(up_hbm, up, w_sem.at[1]),
        pltpu.make_async_copy(down_hbm, down.at[:, pl.ds(1, kk)], w_sem.at[2]),
    ]
    for copy in w_copies:
        copy.start()

    barrier = pltpu.get_barrier_semaphore()
    partners = [dev_y, dev_c, dev_x, dev_z(1), dev_z(2), dev_z(3)]
    for dev in partners:
        pl.semaphore_signal(barrier, inc=1, device_id=dev, device_id_type=MESH_ID)
    pl.semaphore_wait(barrier, len(partners))

    tok_copy.wait()

    raw = send(tok_ref, peer_tok, raw_s.at[0], raw_r.at[0], dev_y)
    raw.start()
    down[:, pl.ds(0, 1)] = jnp.zeros((columns, 1) + down.shape[2:], BF16)
    index = lax.broadcasted_iota(jnp.int32, (width, width), 0)
    parity = index & lax.broadcasted_iota(jnp.int32, (width, width), 1)
    shift = 1
    while shift < width.bit_length():
        parity = parity ^ (parity >> shift)
        shift *= 2
    sign_ref[...] = (1 - 2 * (parity & 1)).astype(F32).astype(BF16)
    for copy in exp_copies:
        copy.wait()
    held = jnp.where(t == 0, held_ref[:, :kk], held_ref[:, kk:])
    block_ids = lax.broadcasted_iota(jnp.int32, slot_vec.shape, 1)
    slot_of = jnp.zeros(slot_vec.shape, jnp.int32)
    for k in range(kk):
        slot_of = jnp.where(held[:, k : k + 1] == block_ids, k + 1, slot_of)
    slot_vec[...] = slot_of
    slot_copy = pltpu.make_async_copy(slot_vec, slot_of_ref, w_sem.at[9])
    slot_copy.start()
    in_limit[...] = jnp.exp2(in_exp_ref[...].astype(F32)).astype(BF16).astype(F32)
    lengths = [lengths_ref[q] for q in range(lengths_ref.shape[0])]
    rows = lax.broadcasted_iota(jnp.int32, (live, slots), 0)
    lane_slots = lax.broadcasted_iota(jnp.int32, (live, slots), 1)

    def pick(group):
        target = slot_target(lengths, lane_slots + group * slots, side)
        return jnp.where(target == rows, 1.0, 0.0).astype(BF16)

    own_rows = jnp.dot(pick(t), tok_ref[...], preferred_element_type=F32)
    other_pick = pick(1 - t)
    raw.wait_recv()
    other_rows = jnp.dot(other_pick, peer_tok[...], preferred_element_type=F32)
    all_tok[f] = (own_rows + other_rows).astype(BF16)

    sent = [raw]

    def start(copy):
        copy.start()
        sent.append(copy)
        return copy

    def rotate_low(g):
        mixed[g] = jnp.dot(all_tok[g], sign_ref[...], preferred_element_type=F32)

    def forward_x(d, g):
        return start(send(all_tok.at[g], all_tok.at[g], agx_s.at[d], agx_r.at[d], dev_x))

    def forward_c(d, g):
        return start(send(all_tok.at[g], all_tok.at[g], agc_s.at[d], agc_r.at[d], dev_c))

    z_copies = [
        start(send(all_tok.at[f], all_tok.at[f], agz_s.at[d - 1], agz_r.at[d - 1], dev_z(d)))
        for d in (1, 2, 3)
    ]
    x_copies = [forward_x(0, f)]
    c_copies = [forward_c(0, f)]
    rotate_low(f)
    for d in (1, 3, 2):
        z_copies[d - 1].wait_recv()
        g = chunk(z_at(4 - d), x, c)
        x_copies.append(forward_x(d, g))
        c_copies.append(forward_c(d, g))
        rotate_low(g)
    for i, d in enumerate((0, 1, 3, 2)):
        x_copies[i].wait_recv()
        g = chunk(z_at(4 - d), 1 - x, c)
        c_copies.append(forward_c(4 + d, g))
        rotate_low(g)
    for i, d in enumerate((0, 1, 3, 2)):
        c_copies[i].wait_recv()
        rotate_low(chunk(z_at(4 - d), x, 1 - c))
    for i, d in enumerate((0, 1, 3, 2)):
        c_copies[4 + i].wait_recv()
        rotate_low(chunk(z_at(4 - d), 1 - x, 1 - c))

    chunks = mixed.shape[0]
    scale = 1.0 / math.sqrt(chunks * width)
    parts = width // 128

    def rotate_high(r, carry):
        at = pl.ds(pl.multiple_of(r * 16, 16), 16)
        for h in range(parts):
            vals = [mixed[i, at, pl.ds(h * 128, 128)] for i in range(chunks)]
            bit = 1
            while bit < chunks:
                nxt = list(vals)
                for i in range(chunks):
                    if not i & bit:
                        nxt[i] = vals[i] + vals[i | bit]
                        nxt[i | bit] = vals[i] - vals[i | bit]
                vals = nxt
                bit *= 2
            for i in range(chunks):
                n = parts * i + h
                limit = in_limit[pl.ds(n, 1), :]
                rotated = (vals[i] * scale).astype(BF16).astype(F32)
                spikes[n, at, :] = jnp.minimum(jnp.maximum(rotated, -limit), limit).astype(BF16)
        return carry

    lax.fori_loop(0, live // 16, rotate_high, 0)

    w_copies[0].wait()
    w_copies[1].wait()

    def pair_sums(j):
        lhs = jnp.concatenate([spikes[gateup_ref[j, t * kk + k]] for k in range(kk)], axis=1)
        rhs = jnp.concatenate([gate[j], up[j]], axis=1)
        return jnp.dot(lhs, rhs, preferred_element_type=F32)

    def gu_copy(i):
        return send(snd_gu.at[i], rcv_gu.at[i], gu_s.at[i], gu_r.at[i], dev_y)

    def rate_copy(i):
        j = t * mine + i
        return send(rate.at[j], rate.at[j], rt_s.at[i], rt_r.at[i], dev_y)

    def give(i, carry):
        snd_gu[i] = pair_sums((1 - t) * mine + i).astype(BF16)
        gu_copy(i).start()
        return carry

    def take(i, carry):
        j = t * mine + i
        own = pair_sums(j)
        gu_copy(i).wait_recv()
        total = own + rcv_gu[i].astype(F32)
        gate_sum = total[:, :128]
        current = gate_sum / (1.0 + jnp.exp(-gate_sum)) * total[:, 128:]
        limit = jnp.exp2(hid_exp_ref[pl.ds(j, 1), :].astype(F32)).astype(BF16).astype(F32)
        rate[j] = jnp.minimum(jnp.maximum(current, -limit), limit).astype(BF16)
        rate_copy(i).start()
        return carry

    lax.fori_loop(0, mine, give, 0)
    lax.fori_loop(0, mine, take, 0)
    w_copies[2].wait()
    slot_copy.wait()
    for i in range(mine):
        rate_copy(i).wait_recv()

    def down_chunk(g):
        lhs = jnp.concatenate([rate[j] for j in range(columns)], axis=1)
        cols = []
        for h in range(parts):
            n = g * parts + h
            cols.append(
                jnp.concatenate([down[j, slot_of_ref[j, n]] for j in range(columns)], axis=0)
            )
        return jnp.dot(lhs, jnp.concatenate(cols, axis=1), preferred_element_type=F32)

    def z_turn(i):
        return z_at(jnp.where(i < 2, 2 + i, 3 - i))

    def core_copy(i):
        return send(snd_c.at[i], rcv_c.at[i], c_s.at[i], c_r.at[i], dev_c)

    half = live // 2
    my_rows = pl.ds(pl.multiple_of(t * half, half), half)
    peer_rows = pl.ds(pl.multiple_of((1 - t) * half, half), half)
    front, back = pl.ds(0, width // 2), pl.ds(width // 2, width // 2)

    def x_copy(i):
        return send(snd_x.at[i], rcv_x.at[i], x_s.at[i], x_r.at[i], dev_x)

    def y_rows_copy(i):
        return send(snd_yr.at[i], rcv_yr.at[i], yr_s.at[i], yr_r.at[i], dev_y)

    def x_rows_copy(i):
        return send(snd_xr.at[i], rcv_xr.at[i], xr_s.at[i], xr_r.at[i], dev_x)

    def give_core_far(i, carry):
        snd_c[i] = down_chunk(chunk(z_turn(i), 1 - x, 1 - c)).astype(BF16)
        core_copy(i).start()
        return carry

    def give_core_near(i, carry):
        snd_c[4 + i] = down_chunk(chunk(z_turn(i), x, 1 - c)).astype(BF16)
        core_copy(4 + i).start()
        return carry

    def give_x(i, carry):
        own = down_chunk(chunk(z_turn(i), 1 - x, c))
        core_copy(i).wait_recv()
        acc[i] = own + rcv_c[i].astype(F32)
        snd_x[i] = acc[i, :, front].astype(BF16)
        x_copy(i).start()
        snd_yr[i] = acc[i, peer_rows, back].astype(BF16)
        y_rows_copy(i).start()
        return carry

    def keep(i, carry):
        own = down_chunk(chunk(z_turn(i), x, c))
        core_copy(4 + i).wait_recv()
        acc[4 + i] = own + rcv_c[4 + i].astype(F32)
        snd_yr[4 + i] = acc[4 + i, peer_rows, back].astype(BF16)
        y_rows_copy(4 + i).start()
        return carry

    def give_x_rows(i, carry):
        y_rows_copy(i).wait_recv()
        snd_xr[i] = (acc[i, my_rows, back] + rcv_yr[i].astype(F32)).astype(BF16)
        x_rows_copy(i).start()
        return carry

    lax.fori_loop(0, 4, give_core_far, 0)
    lax.fori_loop(0, 4, give_x, 0)
    lax.fori_loop(0, 4, give_core_near, 0)
    lax.fori_loop(0, 4, keep, 0)
    lax.fori_loop(0, 4, give_x_rows, 0)

    def front_sum(i):
        x_copy(i).wait_recv()
        return acc[4 + i, :, front] + rcv_x[i].astype(F32)

    def back_sum(i):
        y_rows_copy(4 + i).wait_recv()
        x_rows_copy(i).wait_recv()
        return acc[4 + i, my_rows, back] + rcv_yr[4 + i].astype(F32) + rcv_xr[i].astype(F32)

    def to_z(src, dst, n, d):
        return start(send(src.at[d - 1], dst.at[d - 1], z_s.at[n], z_r.at[n], dev_z(d)))

    zs = []
    zrs = []
    for i, d in enumerate((2, 3, 1)):
        snd_z[d - 1] = front_sum(i).astype(BF16)
        zs.append(to_z(snd_z, rcv_z, d - 1, d))
    front_total = front_sum(3)
    for i, d in enumerate((2, 3, 1)):
        snd_zr[d - 1] = back_sum(i).astype(BF16)
        zrs.append(to_z(snd_zr, rcv_zr, 2 + d, d))
    back_total = back_sum(3)
    for copy, d in zip(zs, (2, 3, 1)):
        copy.wait_recv()
        front_total = front_total + rcv_z[d - 1].astype(F32)
    snd_y[...] = front_total.astype(BF16)
    fin = start(send(snd_y, rcv_y, y_s.at[0], y_r.at[0], dev_y))
    for copy, d in zip(zrs, (2, 3, 1)):
        copy.wait_recv()
        back_total = back_total + rcv_zr[d - 1].astype(F32)
    final[my_rows, :] = back_total.astype(BF16)
    fin_rows = start(send(final.at[my_rows], final.at[my_rows], y_s.at[1], y_r.at[1], dev_y))
    slot_rows = lax.broadcasted_iota(jnp.int32, (slots, live), 0) + t * slots
    live_lanes = lax.broadcasted_iota(jnp.int32, (slots, live), 1)
    place = jnp.where(slot_target(lengths, slot_rows, side) == live_lanes, 1.0, 0.0).astype(BF16)
    fin.wait_recv()
    front_part = (front_total + rcv_y[...].astype(F32)).astype(BF16)
    fin_rows.wait_recv()
    result = jnp.concatenate([front_part, final[...]], axis=1)
    out_ref[...] = jnp.dot(place, result, preferred_element_type=F32).astype(BF16)

    for copy in sent:
        copy.wait_send()
    for i in range(mine):
        gu_copy(i).wait_send()
        rate_copy(i).wait_send()
    for i in range(8):
        core_copy(i).wait_send()
        y_rows_copy(i).wait_send()
    for i in range(4):
        x_copy(i).wait_send()
        x_rows_copy(i).wait_send()


def local_kernel(
    tokens,
    seq_lengths,
    in_exponents,
    hidden_exponents,
    gateup_blocks,
    down_blocks,
    gate_values,
    up_values,
    down_values,
):
    slots, width = tokens.shape
    columns, kk, side, _ = gate_values.shape
    model_width = in_exponents.shape[0]
    blocks = model_width // side
    chunks = model_width // width
    mine = columns // 2
    t = lax.axis_index("tok")
    vmem = pl.BlockSpec(memory_space=pltpu.VMEM)
    anywhere = pl.BlockSpec(memory_space=pl.ANY)
    dma = lambda n: pltpu.SemaphoreType.DMA((n,))
    buf = lambda *shape: pltpu.VMEM(shape, BF16)
    return pl.pallas_call(
        body,
        out_shape=jax.ShapeDtypeStruct((slots, width), BF16),
        in_specs=[anywhere] * 9,
        out_specs=vmem,
        scratch_shapes=[
            pltpu.SMEM(seq_lengths.shape, jnp.int32),
            pltpu.SMEM(gateup_blocks.shape, jnp.int32),
            pltpu.VMEM(down_blocks.shape, jnp.int32),
            pltpu.VMEM((columns, 128), jnp.int32),
            pltpu.SMEM((columns, 128), jnp.int32),
            buf(slots, width),
            pltpu.VMEM((blocks, side), jnp.int32),
            pltpu.VMEM((columns, side), jnp.int32),
            buf(width, width),
            buf(columns, kk * side, side),
            buf(columns, kk * side, side),
            buf(columns, kk + 1, side, side),
            buf(slots, width),
            buf(chunks, slots, width),
            pltpu.VMEM((chunks, slots, width), F32),
            pltpu.VMEM((blocks, side), F32),
            buf(blocks, slots, side),
            buf(mine, slots, 2 * side),
            buf(mine, slots, 2 * side),
            buf(columns, slots, side),
            buf(8, slots, width),
            buf(8, slots, width),
            buf(4, slots, width // 2),
            buf(4, slots, width // 2),
            pltpu.VMEM((8, slots, width), F32),
            buf(slots, width // 2),
            buf(slots, width // 2),
            buf(3, slots, width // 2),
            buf(3, slots, width // 2),
            buf(8, slots // 2, width // 2),
            buf(8, slots // 2, width // 2),
            buf(4, slots // 2, width // 2),
            buf(4, slots // 2, width // 2),
            buf(3, slots // 2, width // 2),
            buf(3, slots // 2, width // 2),
            buf(slots, width // 2),
            dma(10),
            dma(1),
            dma(1),
            dma(3),
            dma(3),
            dma(4),
            dma(4),
            dma(8),
            dma(8),
            dma(mine),
            dma(mine),
            dma(mine),
            dma(mine),
            dma(8),
            dma(8),
            dma(4),
            dma(4),
            dma(2),
            dma(2),
            dma(6),
            dma(6),
            dma(8),
            dma(8),
            dma(4),
            dma(4),
        ],
        compiler_params=pltpu.CompilerParams(
            collective_id=0, has_side_effects=True, vmem_limit_bytes=60 * 1024 * 1024
        ),
        name="spiking_ffn",
    )(
        seq_lengths,
        gateup_blocks,
        down_blocks,
        tokens,
        in_exponents.reshape(blocks, side),
        hidden_exponents.reshape(columns, side),
        gate_values.reshape(columns, kk * side, side),
        up_values.reshape(columns, kk * side, side),
        down_values,
    )


def partner_2(value, axis, stride):
    mask = 2**stride
    pairs = [(source, source ^ mask) for source in range(lax.axis_size(axis))]
    return lax.ppermute(value, axis, pairs)


def sign_table(order_size, value_type):
    indices = jnp.arange(order_size, dtype=jnp.int32)
    shared = indices[:, None] & indices[None, :]
    parity = jnp.zeros((order_size, order_size), jnp.int32)
    for bit_number in range(max(1, (order_size - 1).bit_length())):
        parity = parity ^ shared >> bit_number & 1
    return (1 - 2 * parity).astype(value_type)


def local_general(
    tokens,
    seq_lengths,
    in_exponents,
    hidden_exponents,
    gateup_blocks,
    down_blocks,
    gate_values,
    up_values,
    down_values,
):
    slot_count, feat_local = tokens.shape
    model_width = in_exponents.shape[0]
    seq_width = slot_count // SEQS_DEV
    tok_index = lax.axis_index("tok")
    seq_count = seq_lengths.shape[0]
    earlier = jnp.tril(jnp.ones((seq_count, seq_count), jnp.int32))
    seq_ends = jnp.sum(earlier * seq_lengths[None, :], axis=1)
    seq_starts = seq_ends - seq_lengths
    seq_ids = jnp.arange(seq_lengths.shape[0], dtype=jnp.int32)
    slot_ids = jnp.arange(slot_count, dtype=jnp.int32)
    seq_of = tok_index * SEQS_DEV + slot_ids // seq_width
    position = slot_ids % seq_width
    same_seq = seq_of[:, None] == seq_ids[None, :]
    length_of = jnp.sum(jnp.where(same_seq, seq_lengths[None, :], 0), axis=1)
    start_of = jnp.sum(jnp.where(same_seq, seq_starts[None, :], 0), axis=1)
    live_slot = position < length_of
    pooled = lax.all_gather(tokens, "tok", axis=0, tiled=True)
    wanted = tok_index * seq_width + jnp.arange(seq_width, dtype=jnp.int32)
    owner_seq = jnp.sum((seq_ends[None, :] <= wanted[:, None]).astype(jnp.int32), axis=1)
    owner_match = owner_seq[:, None] == seq_ids[None, :]
    offset = wanted - jnp.sum(jnp.where(owner_match, seq_starts[None, :], 0), axis=1)
    picked_slot = owner_seq * seq_width + offset
    pooled_slots = jnp.arange(pooled.shape[0], dtype=jnp.int32)
    picker = (picked_slot[:, None] == pooled_slots[None, :]).astype(jnp.bfloat16)
    picked = jnp.dot(picker, pooled, preferred_element_type=jnp.float32).astype(jnp.bfloat16)
    row_count = picked.shape[0]
    rotation_scale = 1.0 / math.sqrt(model_width)
    mixed_part = jnp.dot(
        picked, sign_table(feat_local, jnp.bfloat16), preferred_element_type=jnp.float32
    )
    feat_index = lax.axis_index("feat")
    for bit_number in range(lax.axis_size("feat").bit_length() - 1):
        partner = partner_2(mixed_part, "feat", bit_number)
        high_half = feat_index >> bit_number & 1 == 1
        mixed_part = jnp.where(high_half, partner - mixed_part, mixed_part + partner)
    rotated = lax.all_gather(
        (mixed_part * rotation_scale).astype(jnp.bfloat16), "feat", axis=1, tiled=True
    )
    in_limit = jnp.exp2(in_exponents.astype(jnp.float32))
    hidden_limit = jnp.exp2(hidden_exponents.astype(jnp.float32))
    gate_full, up_full, down_full = (
        lax.all_gather(gate_values, "tok", axis=1, tiled=True),
        lax.all_gather(up_values, "tok", axis=1, tiled=True),
        lax.all_gather(down_values, "tok", axis=1, tiled=True),
    )
    block_size = gate_values.shape[2]
    block_count = model_width // block_size
    hidden_local = hidden_exponents.shape[0]
    spike_in = jnp.clip(rotated.astype(jnp.float32), -in_limit, in_limit).astype(jnp.bfloat16)
    block_ids = jnp.arange(block_count, dtype=jnp.int32)
    gateup_place = (gateup_blocks[:, :, None] == block_ids[None, None, :]).astype(jnp.bfloat16)

    def dense(values):
        wide = jnp.einsum(
            "hkbc,hkn->nbhc", values, gateup_place, preferred_element_type=jnp.float32
        )
        return wide.astype(jnp.bfloat16).reshape(model_width, hidden_local)

    gate_sum = jnp.dot(spike_in, dense(gate_full), preferred_element_type=jnp.float32)
    upward = jnp.dot(spike_in, dense(up_full), preferred_element_type=jnp.float32)
    current = jax.nn.silu(gate_sum) * upward
    spiking_rate = jnp.clip(current, -hidden_limit, hidden_limit).astype(jnp.bfloat16)
    indicator = (
        down_blocks[:, :, None] == jnp.arange(block_count, dtype=jnp.int32)[None, None, :]
    ).astype(jnp.bfloat16)
    dense_down_weight = jnp.einsum(
        "hkbc,hkn->hbnc", down_full, indicator, preferred_element_type=jnp.float32
    ).astype(jnp.bfloat16)
    dense_down_weight = dense_down_weight.reshape(hidden_local, model_width)
    partial_block_value = jnp.dot(
        spiking_rate, dense_down_weight, preferred_element_type=jnp.float32
    )
    summed = lax.psum_scatter(partial_block_value, "feat", scatter_dimension=1, tiled=True)
    returned = lax.all_gather(summed.astype(jnp.bfloat16), "tok", axis=0, tiled=True)
    source_row = jnp.where(live_slot, start_of + position, 0)
    returned_rows = jnp.arange(returned.shape[0], dtype=jnp.int32)
    placer = (source_row[:, None] == returned_rows[None, :]) & live_slot[:, None]
    return jnp.dot(
        placer.astype(jnp.bfloat16), returned, preferred_element_type=jnp.float32
    ).astype(jnp.bfloat16)


def solution(mesh):
    in_specs = (
        P("tok", "feat"),
        P(),
        P(),
        P("feat"),
        P("feat", None),
        P("feat", None),
        P("feat", "tok", None, None),
        P("feat", "tok", None, None),
        P("feat", "tok", None, None),
    )
    out_specs = P("tok", "feat")
    same_groups = dict(mesh.shape) == {"tok": 2, "feat": 16}
    local = local_kernel if same_groups else local_general
    return jax.shard_map(local, mesh=mesh, in_specs=in_specs, out_specs=out_specs, check_vma=False)
```

```python
import math

import jax
import jax.numpy as jnp
from jax import lax
from jax.experimental import pallas as pl
from jax.experimental.pallas import tpu as pltpu
from jax.sharding import PartitionSpec as P

SEQS_DEV = 2
MESH_ID = pl.DeviceIdType.MESH
F32 = jnp.float32
BF16 = jnp.bfloat16


def slot_target(lengths, slots, seq_width):
    seq = slots // seq_width
    position = slots % seq_width
    start = jnp.zeros_like(slots)
    length = jnp.zeros_like(slots)
    running = 0
    for q, length_q in enumerate(lengths):
        here = seq == q
        start = jnp.where(here, running, start)
        length = jnp.where(here, length_q, length)
        running = running + length_q
    return jnp.where(position < length, start + position, -1)


def body(
    lengths_hbm,
    gateup_hbm,
    held_hbm,
    tok_hbm,
    in_exp_hbm,
    hid_exp_hbm,
    gate_hbm,
    up_hbm,
    down_hbm,
    out_ref,
    lengths_ref,
    gateup_ref,
    held_ref,
    slot_vec,
    slot_of_ref,
    tok_ref,
    in_exp_ref,
    hid_exp_ref,
    sign_ref,
    gate,
    up,
    down,
    peer_tok,
    all_tok,
    mixed,
    in_limit,
    spikes,
    snd_gu,
    rcv_gu,
    rate,
    snd_c,
    rcv_c,
    snd_x,
    rcv_x,
    acc,
    snd_y,
    rcv_y,
    snd_z,
    rcv_z,
    snd_yr,
    rcv_yr,
    snd_xr,
    rcv_xr,
    snd_zr,
    rcv_zr,
    final,
    w_sem,
    raw_s,
    raw_r,
    agz_s,
    agz_r,
    agx_s,
    agx_r,
    agc_s,
    agc_r,
    gu_s,
    gu_r,
    rt_s,
    rt_r,
    c_s,
    c_r,
    x_s,
    x_r,
    y_s,
    y_r,
    z_s,
    z_r,
    yr_s,
    yr_r,
    xr_s,
    xr_r,
    agy_s,
    agy_r,
):
    t = lax.axis_index("tok")
    f = lax.axis_index("feat")
    z = f // 4
    x = (f // 2) % 2
    c = f % 2
    slots, width = tok_ref.shape
    live = slots
    side = slots // SEQS_DEV
    columns = rate.shape[0]
    mine = columns // 2
    kk = down.shape[1] - 1

    dev_y = (1 - t, f)
    dev_c = (t, f + 1 - 2 * c)
    dev_x = (t, f + 2 - 4 * x)

    def z_at(d):
        return lax.rem(z + d, 4)

    def dev_z(d):
        return (t, z_at(d) * 4 + x * 2 + c)

    def chunk(zz, xx, cc):
        return zz * 4 + xx * 2 + cc

    def send(src, dst, ssem, rsem, dev):
        return pltpu.make_async_remote_copy(
            src_ref=src,
            dst_ref=dst,
            send_sem=ssem,
            recv_sem=rsem,
            device_id=dev,
            device_id_type=MESH_ID,
        )

    tok_copy = pltpu.make_async_copy(tok_hbm, tok_ref, w_sem.at[3])
    exp_copies = [
        pltpu.make_async_copy(in_exp_hbm, in_exp_ref, w_sem.at[4]),
        pltpu.make_async_copy(hid_exp_hbm, hid_exp_ref, w_sem.at[5]),
        pltpu.make_async_copy(lengths_hbm, lengths_ref, w_sem.at[6]),
        pltpu.make_async_copy(gateup_hbm, gateup_ref, w_sem.at[7]),
        pltpu.make_async_copy(held_hbm, held_ref, w_sem.at[8]),
    ]
    tok_copy.start()
    for copy in exp_copies:
        copy.start()
    w_copies = [
        pltpu.make_async_copy(gate_hbm, gate, w_sem.at[0]),
        pltpu.make_async_copy(up_hbm, up, w_sem.at[1]),
        pltpu.make_async_copy(down_hbm, down.at[:, pl.ds(1, kk)], w_sem.at[2]),
    ]
    for copy in w_copies:
        copy.start()

    barrier = pltpu.get_barrier_semaphore()
    partners = [dev_y, dev_c, dev_x, dev_z(1), dev_z(2), dev_z(3)]
    for dev in partners:
        pl.semaphore_signal(barrier, inc=1, device_id=dev, device_id_type=MESH_ID)
    pl.semaphore_wait(barrier, len(partners))

    tok_copy.wait()

    raw = send(tok_ref, peer_tok, raw_s.at[0], raw_r.at[0], dev_y)
    raw.start()
    down[:, pl.ds(0, 1)] = jnp.zeros((columns, 1) + down.shape[2:], BF16)
    index = lax.broadcasted_iota(jnp.int32, (width, width), 0)
    parity = index & lax.broadcasted_iota(jnp.int32, (width, width), 1)
    shift = 1
    while shift < width.bit_length():
        parity = parity ^ (parity >> shift)
        shift *= 2
    sign_ref[...] = (1 - 2 * (parity & 1)).astype(F32).astype(BF16)
    for copy in exp_copies:
        copy.wait()
    held = jnp.where(t == 0, held_ref[:, :kk], held_ref[:, kk:])
    block_ids = lax.broadcasted_iota(jnp.int32, slot_vec.shape, 1)
    slot_of = jnp.zeros(slot_vec.shape, jnp.int32)
    for k in range(kk):
        slot_of = jnp.where(held[:, k : k + 1] == block_ids, k + 1, slot_of)
    slot_vec[...] = slot_of
    slot_copy = pltpu.make_async_copy(slot_vec, slot_of_ref, w_sem.at[9])
    slot_copy.start()
    in_limit[...] = jnp.exp2(in_exp_ref[...].astype(F32)).astype(BF16).astype(F32)
    lengths = [lengths_ref[q] for q in range(lengths_ref.shape[0])]
    rows = lax.broadcasted_iota(jnp.int32, (live, slots), 0)
    lane_slots = lax.broadcasted_iota(jnp.int32, (live, slots), 1)

    def pick(group):
        target = slot_target(lengths, lane_slots + group * slots, side)
        return jnp.where(target == rows, 1.0, 0.0).astype(BF16)

    own_rows = jnp.dot(pick(t), tok_ref[...], preferred_element_type=F32)
    other_pick = pick(1 - t)
    raw.wait_recv()
    other_rows = jnp.dot(other_pick, peer_tok[...], preferred_element_type=F32)
    all_tok[f] = (own_rows + other_rows).astype(BF16)

    sent = [raw]

    def start(copy):
        copy.start()
        sent.append(copy)
        return copy

    def rotate_low(g):
        mixed[g] = jnp.dot(all_tok[g], sign_ref[...], preferred_element_type=F32)

    def forward_x(d, g):
        return start(send(all_tok.at[g], all_tok.at[g], agx_s.at[d], agx_r.at[d], dev_x))

    def forward_c(d, g):
        return start(send(all_tok.at[g], all_tok.at[g], agc_s.at[d], agc_r.at[d], dev_c))

    half = live // 2
    my_rows = pl.ds(pl.multiple_of(t * half, half), half)

    def half_copy(g, ssem, rsem, dev):
        return start(send(all_tok.at[g, my_rows], all_tok.at[g, my_rows], ssem, rsem, dev))

    z_copies = [
        half_copy(f, agz_s.at[d - 1], agz_r.at[d - 1], dev_z(d)) for d in (1, 2, 3)
    ]
    x_copies = [forward_x(0, f)]
    c_copies = [forward_c(0, f)]
    rotate_low(f)
    y_copies = []
    for d in (1, 3, 2):
        z_copies[d - 1].wait_recv()
        g = chunk(z_at(4 - d), x, c)
        y_copies.append(half_copy(g, agy_s.at[d - 1], agy_r.at[d - 1], dev_y))
    for i, d in enumerate((1, 3, 2)):
        y_copies[i].wait_recv()
        g = chunk(z_at(4 - d), x, c)
        x_copies.append(forward_x(d, g))
        c_copies.append(forward_c(d, g))
        rotate_low(g)
    for i, d in enumerate((0, 1, 3, 2)):
        x_copies[i].wait_recv()
        g = chunk(z_at(4 - d), 1 - x, c)
        c_copies.append(forward_c(4 + d, g))
        rotate_low(g)
    for i, d in enumerate((0, 1, 3, 2)):
        c_copies[i].wait_recv()
        rotate_low(chunk(z_at(4 - d), x, 1 - c))
    for i, d in enumerate((0, 1, 3, 2)):
        c_copies[4 + i].wait_recv()
        rotate_low(chunk(z_at(4 - d), 1 - x, 1 - c))

    chunks = mixed.shape[0]
    scale = 1.0 / math.sqrt(chunks * width)
    parts = width // 128

    def rotate_high(r, carry):
        at = pl.ds(pl.multiple_of(r * 16, 16), 16)
        for h in range(parts):
            vals = [mixed[i, at, pl.ds(h * 128, 128)] for i in range(chunks)]
            bit = 1
            while bit < chunks:
                nxt = list(vals)
                for i in range(chunks):
                    if not i & bit:
                        nxt[i] = vals[i] + vals[i | bit]
                        nxt[i | bit] = vals[i] - vals[i | bit]
                vals = nxt
                bit *= 2
            for i in range(chunks):
                n = parts * i + h
                limit = in_limit[pl.ds(n, 1), :]
                rotated = (vals[i] * scale).astype(BF16).astype(F32)
                spikes[n, at, :] = jnp.minimum(jnp.maximum(rotated, -limit), limit).astype(BF16)
        return carry

    lax.fori_loop(0, live // 16, rotate_high, 0)

    w_copies[0].wait()
    w_copies[1].wait()

    def pair_sums(j):
        lhs = jnp.concatenate([spikes[gateup_ref[j, t * kk + k]] for k in range(kk)], axis=1)
        rhs = jnp.concatenate([gate[j], up[j]], axis=1)
        return jnp.dot(lhs, rhs, preferred_element_type=F32)

    def gu_copy(i):
        return send(snd_gu.at[i], rcv_gu.at[i], gu_s.at[i], gu_r.at[i], dev_y)

    def rate_copy(i):
        j = t * mine + i
        return send(rate.at[j], rate.at[j], rt_s.at[i], rt_r.at[i], dev_y)

    def give(i, carry):
        snd_gu[i] = pair_sums((1 - t) * mine + i).astype(BF16)
        gu_copy(i).start()
        return carry

    def take(i, carry):
        j = t * mine + i
        own = pair_sums(j)
        gu_copy(i).wait_recv()
        total = own + rcv_gu[i].astype(F32)
        gate_sum = total[:, :128]
        current = gate_sum / (1.0 + jnp.exp(-gate_sum)) * total[:, 128:]
        limit = jnp.exp2(hid_exp_ref[pl.ds(j, 1), :].astype(F32)).astype(BF16).astype(F32)
        rate[j] = jnp.minimum(jnp.maximum(current, -limit), limit).astype(BF16)
        rate_copy(i).start()
        return carry

    lax.fori_loop(0, mine, give, 0)
    lax.fori_loop(0, mine, take, 0)
    w_copies[2].wait()
    slot_copy.wait()
    for i in range(mine):
        rate_copy(i).wait_recv()

    def down_chunk(g):
        lhs = jnp.concatenate([rate[j] for j in range(columns)], axis=1)
        cols = []
        for h in range(parts):
            n = g * parts + h
            cols.append(
                jnp.concatenate([down[j, slot_of_ref[j, n]] for j in range(columns)], axis=0)
            )
        return jnp.dot(lhs, jnp.concatenate(cols, axis=1), preferred_element_type=F32)

    def z_turn(i):
        return z_at(jnp.where(i < 2, 2 + i, 3 - i))

    def core_copy(i):
        return send(snd_c.at[i], rcv_c.at[i], c_s.at[i], c_r.at[i], dev_c)

    peer_rows = pl.ds(pl.multiple_of((1 - t) * half, half), half)
    front, back = pl.ds(0, width // 2), pl.ds(width // 2, width // 2)

    def x_copy(i):
        return send(snd_x.at[i], rcv_x.at[i], x_s.at[i], x_r.at[i], dev_x)

    def y_rows_copy(i):
        return send(snd_yr.at[i], rcv_yr.at[i], yr_s.at[i], yr_r.at[i], dev_y)

    def x_rows_copy(i):
        return send(snd_xr.at[i], rcv_xr.at[i], xr_s.at[i], xr_r.at[i], dev_x)

    def give_core_far(i, carry):
        snd_c[i] = down_chunk(chunk(z_turn(i), 1 - x, 1 - c)).astype(BF16)
        core_copy(i).start()
        return carry

    def give_core_near(i, carry):
        snd_c[4 + i] = down_chunk(chunk(z_turn(i), x, 1 - c)).astype(BF16)
        core_copy(4 + i).start()
        return carry

    def give_x(i, carry):
        own = down_chunk(chunk(z_turn(i), 1 - x, c))
        core_copy(i).wait_recv()
        acc[i] = own + rcv_c[i].astype(F32)
        snd_x[i] = acc[i, :, front].astype(BF16)
        x_copy(i).start()
        snd_yr[i] = acc[i, peer_rows, back].astype(BF16)
        y_rows_copy(i).start()
        return carry

    def keep(i, carry):
        own = down_chunk(chunk(z_turn(i), x, c))
        core_copy(4 + i).wait_recv()
        acc[4 + i] = own + rcv_c[4 + i].astype(F32)
        snd_yr[4 + i] = acc[4 + i, peer_rows, back].astype(BF16)
        y_rows_copy(4 + i).start()
        return carry

    def give_x_rows(i, carry):
        y_rows_copy(i).wait_recv()
        snd_xr[i] = (acc[i, my_rows, back] + rcv_yr[i].astype(F32)).astype(BF16)
        x_rows_copy(i).start()
        return carry

    lax.fori_loop(0, 4, give_core_far, 0)
    lax.fori_loop(0, 4, give_x, 0)
    lax.fori_loop(0, 4, give_core_near, 0)
    lax.fori_loop(0, 4, keep, 0)
    lax.fori_loop(0, 4, give_x_rows, 0)

    def front_sum(i):
        x_copy(i).wait_recv()
        return acc[4 + i, :, front] + rcv_x[i].astype(F32)

    def back_sum(i):
        y_rows_copy(4 + i).wait_recv()
        x_rows_copy(i).wait_recv()
        return acc[4 + i, my_rows, back] + rcv_yr[4 + i].astype(F32) + rcv_xr[i].astype(F32)

    def to_z(src, dst, n, d):
        return start(send(src.at[d - 1], dst.at[d - 1], z_s.at[n], z_r.at[n], dev_z(d)))

    zs = []
    zrs = []
    for i, d in enumerate((2, 3, 1)):
        snd_z[d - 1] = front_sum(i).astype(BF16)
        zs.append(to_z(snd_z, rcv_z, d - 1, d))
    front_total = front_sum(3)
    for i, d in enumerate((2, 3, 1)):
        snd_zr[d - 1] = back_sum(i).astype(BF16)
        zrs.append(to_z(snd_zr, rcv_zr, 2 + d, d))
    back_total = back_sum(3)
    for copy, d in zip(zs, (2, 3, 1)):
        copy.wait_recv()
        front_total = front_total + rcv_z[d - 1].astype(F32)
    snd_y[...] = front_total.astype(BF16)
    fin = start(send(snd_y, rcv_y, y_s.at[0], y_r.at[0], dev_y))
    for copy, d in zip(zrs, (2, 3, 1)):
        copy.wait_recv()
        back_total = back_total + rcv_zr[d - 1].astype(F32)
    final[my_rows, :] = back_total.astype(BF16)
    fin_rows = start(send(final.at[my_rows], final.at[my_rows], y_s.at[1], y_r.at[1], dev_y))
    slot_rows = lax.broadcasted_iota(jnp.int32, (slots, live), 0) + t * slots
    live_lanes = lax.broadcasted_iota(jnp.int32, (slots, live), 1)
    place = jnp.where(slot_target(lengths, slot_rows, side) == live_lanes, 1.0, 0.0).astype(BF16)
    fin.wait_recv()
    front_part = (front_total + rcv_y[...].astype(F32)).astype(BF16)
    fin_rows.wait_recv()
    result = jnp.concatenate([front_part, final[...]], axis=1)
    out_ref[...] = jnp.dot(place, result, preferred_element_type=F32).astype(BF16)

    for copy in sent:
        copy.wait_send()
    for i in range(mine):
        gu_copy(i).wait_send()
        rate_copy(i).wait_send()
    for i in range(8):
        core_copy(i).wait_send()
        y_rows_copy(i).wait_send()
    for i in range(4):
        x_copy(i).wait_send()
        x_rows_copy(i).wait_send()


def local_kernel(
    tokens,
    seq_lengths,
    in_exponents,
    hidden_exponents,
    gateup_blocks,
    down_blocks,
    gate_values,
    up_values,
    down_values,
):
    slots, width = tokens.shape
    columns, kk, side, _ = gate_values.shape
    model_width = in_exponents.shape[0]
    blocks = model_width // side
    chunks = model_width // width
    mine = columns // 2
    t = lax.axis_index("tok")
    vmem = pl.BlockSpec(memory_space=pltpu.VMEM)
    anywhere = pl.BlockSpec(memory_space=pl.ANY)
    dma = lambda n: pltpu.SemaphoreType.DMA((n,))
    buf = lambda *shape: pltpu.VMEM(shape, BF16)
    return pl.pallas_call(
        body,
        out_shape=jax.ShapeDtypeStruct((slots, width), BF16),
        in_specs=[anywhere] * 9,
        out_specs=vmem,
        scratch_shapes=[
            pltpu.SMEM(seq_lengths.shape, jnp.int32),
            pltpu.SMEM(gateup_blocks.shape, jnp.int32),
            pltpu.VMEM(down_blocks.shape, jnp.int32),
            pltpu.VMEM((columns, 128), jnp.int32),
            pltpu.SMEM((columns, 128), jnp.int32),
            buf(slots, width),
            pltpu.VMEM((blocks, side), jnp.int32),
            pltpu.VMEM((columns, side), jnp.int32),
            buf(width, width),
            buf(columns, kk * side, side),
            buf(columns, kk * side, side),
            buf(columns, kk + 1, side, side),
            buf(slots, width),
            buf(chunks, slots, width),
            pltpu.VMEM((chunks, slots, width), F32),
            pltpu.VMEM((blocks, side), F32),
            buf(blocks, slots, side),
            buf(mine, slots, 2 * side),
            buf(mine, slots, 2 * side),
            buf(columns, slots, side),
            buf(8, slots, width),
            buf(8, slots, width),
            buf(4, slots, width // 2),
            buf(4, slots, width // 2),
            pltpu.VMEM((8, slots, width), F32),
            buf(slots, width // 2),
            buf(slots, width // 2),
            buf(3, slots, width // 2),
            buf(3, slots, width // 2),
            buf(8, slots // 2, width // 2),
            buf(8, slots // 2, width // 2),
            buf(4, slots // 2, width // 2),
            buf(4, slots // 2, width // 2),
            buf(3, slots // 2, width // 2),
            buf(3, slots // 2, width // 2),
            buf(slots, width // 2),
            dma(10),
            dma(1),
            dma(1),
            dma(3),
            dma(3),
            dma(4),
            dma(4),
            dma(8),
            dma(8),
            dma(mine),
            dma(mine),
            dma(mine),
            dma(mine),
            dma(8),
            dma(8),
            dma(4),
            dma(4),
            dma(2),
            dma(2),
            dma(6),
            dma(6),
            dma(8),
            dma(8),
            dma(4),
            dma(4),
            dma(3),
            dma(3),
        ],
        compiler_params=pltpu.CompilerParams(
            collective_id=0, has_side_effects=True, vmem_limit_bytes=60 * 1024 * 1024
        ),
        name="spiking_ffn",
    )(
        seq_lengths,
        gateup_blocks,
        down_blocks,
        tokens,
        in_exponents.reshape(blocks, side),
        hidden_exponents.reshape(columns, side),
        gate_values.reshape(columns, kk * side, side),
        up_values.reshape(columns, kk * side, side),
        down_values,
    )


def partner_2(value, axis, stride):
    mask = 2**stride
    pairs = [(source, source ^ mask) for source in range(lax.axis_size(axis))]
    return lax.ppermute(value, axis, pairs)


def sign_table(order_size, value_type):
    indices = jnp.arange(order_size, dtype=jnp.int32)
    shared = indices[:, None] & indices[None, :]
    parity = jnp.zeros((order_size, order_size), jnp.int32)
    for bit_number in range(max(1, (order_size - 1).bit_length())):
        parity = parity ^ shared >> bit_number & 1
    return (1 - 2 * parity).astype(value_type)


def local_general(
    tokens,
    seq_lengths,
    in_exponents,
    hidden_exponents,
    gateup_blocks,
    down_blocks,
    gate_values,
    up_values,
    down_values,
):
    slot_count, feat_local = tokens.shape
    model_width = in_exponents.shape[0]
    seq_width = slot_count // SEQS_DEV
    tok_index = lax.axis_index("tok")
    seq_count = seq_lengths.shape[0]
    earlier = jnp.tril(jnp.ones((seq_count, seq_count), jnp.int32))
    seq_ends = jnp.sum(earlier * seq_lengths[None, :], axis=1)
    seq_starts = seq_ends - seq_lengths
    seq_ids = jnp.arange(seq_lengths.shape[0], dtype=jnp.int32)
    slot_ids = jnp.arange(slot_count, dtype=jnp.int32)
    seq_of = tok_index * SEQS_DEV + slot_ids // seq_width
    position = slot_ids % seq_width
    same_seq = seq_of[:, None] == seq_ids[None, :]
    length_of = jnp.sum(jnp.where(same_seq, seq_lengths[None, :], 0), axis=1)
    start_of = jnp.sum(jnp.where(same_seq, seq_starts[None, :], 0), axis=1)
    live_slot = position < length_of
    pooled = lax.all_gather(tokens, "tok", axis=0, tiled=True)
    wanted = tok_index * seq_width + jnp.arange(seq_width, dtype=jnp.int32)
    owner_seq = jnp.sum((seq_ends[None, :] <= wanted[:, None]).astype(jnp.int32), axis=1)
    owner_match = owner_seq[:, None] == seq_ids[None, :]
    offset = wanted - jnp.sum(jnp.where(owner_match, seq_starts[None, :], 0), axis=1)
    picked_slot = owner_seq * seq_width + offset
    pooled_slots = jnp.arange(pooled.shape[0], dtype=jnp.int32)
    picker = (picked_slot[:, None] == pooled_slots[None, :]).astype(jnp.bfloat16)
    picked = jnp.dot(picker, pooled, preferred_element_type=jnp.float32).astype(jnp.bfloat16)
    row_count = picked.shape[0]
    rotation_scale = 1.0 / math.sqrt(model_width)
    mixed_part = jnp.dot(
        picked, sign_table(feat_local, jnp.bfloat16), preferred_element_type=jnp.float32
    )
    feat_index = lax.axis_index("feat")
    for bit_number in range(lax.axis_size("feat").bit_length() - 1):
        partner = partner_2(mixed_part, "feat", bit_number)
        high_half = feat_index >> bit_number & 1 == 1
        mixed_part = jnp.where(high_half, partner - mixed_part, mixed_part + partner)
    rotated = lax.all_gather(
        (mixed_part * rotation_scale).astype(jnp.bfloat16), "feat", axis=1, tiled=True
    )
    in_limit = jnp.exp2(in_exponents.astype(jnp.float32))
    hidden_limit = jnp.exp2(hidden_exponents.astype(jnp.float32))
    gate_full, up_full, down_full = (
        lax.all_gather(gate_values, "tok", axis=1, tiled=True),
        lax.all_gather(up_values, "tok", axis=1, tiled=True),
        lax.all_gather(down_values, "tok", axis=1, tiled=True),
    )
    block_size = gate_values.shape[2]
    block_count = model_width // block_size
    hidden_local = hidden_exponents.shape[0]
    spike_in = jnp.clip(rotated.astype(jnp.float32), -in_limit, in_limit).astype(jnp.bfloat16)
    block_ids = jnp.arange(block_count, dtype=jnp.int32)
    gateup_place = (gateup_blocks[:, :, None] == block_ids[None, None, :]).astype(jnp.bfloat16)

    def dense(values):
        wide = jnp.einsum(
            "hkbc,hkn->nbhc", values, gateup_place, preferred_element_type=jnp.float32
        )
        return wide.astype(jnp.bfloat16).reshape(model_width, hidden_local)

    gate_sum = jnp.dot(spike_in, dense(gate_full), preferred_element_type=jnp.float32)
    upward = jnp.dot(spike_in, dense(up_full), preferred_element_type=jnp.float32)
    current = jax.nn.silu(gate_sum) * upward
    spiking_rate = jnp.clip(current, -hidden_limit, hidden_limit).astype(jnp.bfloat16)
    indicator = (
        down_blocks[:, :, None] == jnp.arange(block_count, dtype=jnp.int32)[None, None, :]
    ).astype(jnp.bfloat16)
    dense_down_weight = jnp.einsum(
        "hkbc,hkn->hbnc", down_full, indicator, preferred_element_type=jnp.float32
    ).astype(jnp.bfloat16)
    dense_down_weight = dense_down_weight.reshape(hidden_local, model_width)
    partial_block_value = jnp.dot(
        spiking_rate, dense_down_weight, preferred_element_type=jnp.float32
    )
    summed = lax.psum_scatter(partial_block_value, "feat", scatter_dimension=1, tiled=True)
    returned = lax.all_gather(summed.astype(jnp.bfloat16), "tok", axis=0, tiled=True)
    source_row = jnp.where(live_slot, start_of + position, 0)
    returned_rows = jnp.arange(returned.shape[0], dtype=jnp.int32)
    placer = (source_row[:, None] == returned_rows[None, :]) & live_slot[:, None]
    return jnp.dot(
        placer.astype(jnp.bfloat16), returned, preferred_element_type=jnp.float32
    ).astype(jnp.bfloat16)


def solution(mesh):
    in_specs = (
        P("tok", "feat"),
        P(),
        P(),
        P("feat"),
        P("feat", None),
        P("feat", None),
        P("feat", "tok", None, None),
        P("feat", "tok", None, None),
        P("feat", "tok", None, None),
    )
    out_specs = P("tok", "feat")
    same_groups = dict(mesh.shape) == {"tok": 2, "feat": 16}
    local = local_kernel if same_groups else local_general
    return jax.shard_map(local, mesh=mesh, in_specs=in_specs, out_specs=out_specs, check_vma=False)
```

```python
import math

import jax
import jax.numpy as jnp
from jax import lax
from jax.experimental import pallas as pl
from jax.experimental.pallas import tpu as pltpu
from jax.sharding import PartitionSpec as P

SEQS_DEV = 2
MESH_ID = pl.DeviceIdType.MESH
F32 = jnp.float32
BF16 = jnp.bfloat16


def slot_target(lengths, slots, seq_width):
    seq = slots // seq_width
    position = slots % seq_width
    start = jnp.zeros_like(slots)
    length = jnp.zeros_like(slots)
    running = 0
    for q, length_q in enumerate(lengths):
        here = seq == q
        start = jnp.where(here, running, start)
        length = jnp.where(here, length_q, length)
        running = running + length_q
    return jnp.where(position < length, start + position, -1)


def body(
    lengths_hbm,
    gateup_hbm,
    held_hbm,
    tok_hbm,
    in_exp_hbm,
    hid_exp_hbm,
    gate_hbm,
    up_hbm,
    down_hbm,
    out_ref,
    lengths_ref,
    gateup_ref,
    held_ref,
    slot_vec,
    slot_of_ref,
    tok_ref,
    in_exp_ref,
    hid_exp_ref,
    sign_ref,
    gate,
    up,
    down,
    peer_tok,
    all_tok,
    mixed,
    in_limit,
    spikes,
    snd_gu,
    rcv_gu,
    rate,
    snd_c,
    rcv_c,
    snd_x,
    rcv_x,
    acc,
    snd_y,
    rcv_y,
    snd_z,
    rcv_z,
    snd_yr,
    rcv_yr,
    snd_xr,
    rcv_xr,
    snd_zr,
    rcv_zr,
    final,
    w_sem,
    raw_s,
    raw_r,
    agz_s,
    agz_r,
    agx_s,
    agx_r,
    agc_s,
    agc_r,
    gu_s,
    gu_r,
    rt_s,
    rt_r,
    c_s,
    c_r,
    x_s,
    x_r,
    y_s,
    y_r,
    z_s,
    z_r,
    yr_s,
    yr_r,
    xr_s,
    xr_r,
):
    t = lax.axis_index("tok")
    f = lax.axis_index("feat")
    z = f // 4
    x = (f // 2) % 2
    c = f % 2
    slots, width = tok_ref.shape
    live = slots
    side = slots // SEQS_DEV
    columns = rate.shape[0]
    mine = columns // 2
    kk = down.shape[1] - 1

    dev_y = (1 - t, f)
    dev_c = (t, f + 1 - 2 * c)
    dev_x = (t, f + 2 - 4 * x)

    def z_at(d):
        return lax.rem(z + d, 4)

    def dev_z(d):
        return (t, z_at(d) * 4 + x * 2 + c)

    def chunk(zz, xx, cc):
        return zz * 4 + xx * 2 + cc

    def send(src, dst, ssem, rsem, dev):
        return pltpu.make_async_remote_copy(
            src_ref=src,
            dst_ref=dst,
            send_sem=ssem,
            recv_sem=rsem,
            device_id=dev,
            device_id_type=MESH_ID,
        )

    tok_copy = pltpu.make_async_copy(tok_hbm, tok_ref, w_sem.at[3])
    exp_copies = [
        pltpu.make_async_copy(in_exp_hbm, in_exp_ref, w_sem.at[4]),
        pltpu.make_async_copy(hid_exp_hbm, hid_exp_ref, w_sem.at[5]),
        pltpu.make_async_copy(lengths_hbm, lengths_ref, w_sem.at[6]),
        pltpu.make_async_copy(gateup_hbm, gateup_ref, w_sem.at[7]),
        pltpu.make_async_copy(held_hbm, held_ref, w_sem.at[8]),
    ]
    tok_copy.start()
    for copy in exp_copies:
        copy.start()
    w_copies = [
        pltpu.make_async_copy(gate_hbm, gate, w_sem.at[0]),
        pltpu.make_async_copy(up_hbm, up, w_sem.at[1]),
        pltpu.make_async_copy(down_hbm, down.at[:, pl.ds(1, kk)], w_sem.at[2]),
    ]
    for copy in w_copies:
        copy.start()

    barrier = pltpu.get_barrier_semaphore()
    partners = [dev_y, dev_c, dev_x, dev_z(1), dev_z(2), dev_z(3)]
    for dev in partners:
        pl.semaphore_signal(barrier, inc=1, device_id=dev, device_id_type=MESH_ID)
    pl.semaphore_wait(barrier, len(partners))

    tok_copy.wait()

    raw = send(tok_ref, peer_tok, raw_s.at[0], raw_r.at[0], dev_y)
    raw.start()
    down[:, pl.ds(0, 1)] = jnp.zeros((columns, 1) + down.shape[2:], BF16)
    index = lax.broadcasted_iota(jnp.int32, (width, width), 0)
    parity = index & lax.broadcasted_iota(jnp.int32, (width, width), 1)
    shift = 1
    while shift < width.bit_length():
        parity = parity ^ (parity >> shift)
        shift *= 2
    sign_ref[...] = (1 - 2 * (parity & 1)).astype(F32).astype(BF16)
    for copy in exp_copies:
        copy.wait()
    held = jnp.where(t == 0, held_ref[:, :kk], held_ref[:, kk:])
    block_ids = lax.broadcasted_iota(jnp.int32, slot_vec.shape, 1)
    slot_of = jnp.zeros(slot_vec.shape, jnp.int32)
    for k in range(kk):
        slot_of = jnp.where(held[:, k : k + 1] == block_ids, k + 1, slot_of)
    slot_vec[...] = slot_of
    slot_copy = pltpu.make_async_copy(slot_vec, slot_of_ref, w_sem.at[9])
    slot_copy.start()
    in_limit[...] = jnp.exp2(in_exp_ref[...].astype(F32)).astype(BF16).astype(F32)
    lengths = [lengths_ref[q] for q in range(lengths_ref.shape[0])]
    rows = lax.broadcasted_iota(jnp.int32, (live, slots), 0)
    lane_slots = lax.broadcasted_iota(jnp.int32, (live, slots), 1)

    def pick(group):
        target = slot_target(lengths, lane_slots + group * slots, side)
        return jnp.where(target == rows, 1.0, 0.0).astype(BF16)

    own_rows = jnp.dot(pick(t), tok_ref[...], preferred_element_type=F32)
    other_pick = pick(1 - t)
    raw.wait_recv()
    other_rows = jnp.dot(other_pick, peer_tok[...], preferred_element_type=F32)
    all_tok[f] = (own_rows + other_rows).astype(BF16)

    sent = [raw]

    def start(copy):
        copy.start()
        sent.append(copy)
        return copy

    def rotate_low(g):
        mixed[g] = jnp.dot(all_tok[g], sign_ref[...], preferred_element_type=F32)

    def forward_x(d, g):
        return start(send(all_tok.at[g], all_tok.at[g], agx_s.at[d], agx_r.at[d], dev_x))

    def forward_c(d, g):
        return start(send(all_tok.at[g], all_tok.at[g], agc_s.at[d], agc_r.at[d], dev_c))

    z_copies = [
        start(send(all_tok.at[f], all_tok.at[f], agz_s.at[d - 1], agz_r.at[d - 1], dev_z(d)))
        for d in (1, 2, 3)
    ]
    x_copies = [forward_x(0, f)]
    c_copies = [forward_c(0, f)]
    rotate_low(f)
    for d in (1, 3, 2):
        z_copies[d - 1].wait_recv()
        g = chunk(z_at(4 - d), x, c)
        x_copies.append(forward_x(d, g))
        c_copies.append(forward_c(d, g))
        rotate_low(g)
    for i, d in enumerate((0, 1, 3, 2)):
        x_copies[i].wait_recv()
        g = chunk(z_at(4 - d), 1 - x, c)
        c_copies.append(forward_c(4 + d, g))
        rotate_low(g)
    for i, d in enumerate((0, 1, 3, 2)):
        c_copies[i].wait_recv()
        rotate_low(chunk(z_at(4 - d), x, 1 - c))
    for i, d in enumerate((0, 1, 3, 2)):
        c_copies[4 + i].wait_recv()
        rotate_low(chunk(z_at(4 - d), 1 - x, 1 - c))

    chunks = mixed.shape[0]
    scale = 1.0 / math.sqrt(chunks * width)
    parts = width // 128

    def rotate_high(r, carry):
        at = pl.ds(pl.multiple_of(r * 16, 16), 16)
        for h in range(parts):
            vals = [mixed[i, at, pl.ds(h * 128, 128)] for i in range(chunks)]
            bit = 1
            while bit < chunks:
                nxt = list(vals)
                for i in range(chunks):
                    if not i & bit:
                        nxt[i] = vals[i] + vals[i | bit]
                        nxt[i | bit] = vals[i] - vals[i | bit]
                vals = nxt
                bit *= 2
            for i in range(chunks):
                n = parts * i + h
                limit = in_limit[pl.ds(n, 1), :]
                rotated = (vals[i] * scale).astype(BF16).astype(F32)
                spikes[n, at, :] = jnp.minimum(jnp.maximum(rotated, -limit), limit).astype(BF16)
        return carry

    lax.fori_loop(0, live // 16, rotate_high, 0)

    w_copies[0].wait()
    w_copies[1].wait()

    def pair_sums(j):
        lhs = jnp.concatenate([spikes[gateup_ref[j, t * kk + k]] for k in range(kk)], axis=1)
        rhs = jnp.concatenate([gate[j], up[j]], axis=1)
        return jnp.dot(lhs, rhs, preferred_element_type=F32)

    def gu_copy(i):
        return send(snd_gu.at[i], rcv_gu.at[i], gu_s.at[i], gu_r.at[i], dev_y)

    def rate_copy(i):
        j = t * mine + i
        return send(rate.at[j], rate.at[j], rt_s.at[i], rt_r.at[i], dev_y)

    def give(i, carry):
        snd_gu[i] = pair_sums((1 - t) * mine + i).astype(BF16)
        gu_copy(i).start()
        return carry

    def take(i, carry):
        j = t * mine + i
        own = pair_sums(j)
        gu_copy(i).wait_recv()
        total = own + rcv_gu[i].astype(F32)
        gate_sum = total[:, :128]
        current = gate_sum / (1.0 + jnp.exp(-gate_sum)) * total[:, 128:]
        limit = jnp.exp2(hid_exp_ref[pl.ds(j, 1), :].astype(F32)).astype(BF16).astype(F32)
        rate[j] = jnp.minimum(jnp.maximum(current, -limit), limit).astype(BF16)
        rate_copy(i).start()
        return carry

    lax.fori_loop(0, mine, give, 0)
    lax.fori_loop(0, mine, take, 0)
    w_copies[2].wait()
    slot_copy.wait()
    for i in range(mine):
        rate_copy(i).wait_recv()

    def down_chunk(g):
        lhs = jnp.concatenate([rate[j] for j in range(columns)], axis=1)
        cols = []
        for h in range(parts):
            n = g * parts + h
            cols.append(
                jnp.concatenate([down[j, slot_of_ref[j, n]] for j in range(columns)], axis=0)
            )
        return jnp.dot(lhs, jnp.concatenate(cols, axis=1), preferred_element_type=F32)

    def z_turn(i):
        return z_at(jnp.where(i < 2, 2 + i, 3 - i))

    def core_copy(i):
        return send(snd_c.at[i], rcv_c.at[i], c_s.at[i], c_r.at[i], dev_c)

    half = live // 2
    my_rows = pl.ds(pl.multiple_of(t * half, half), half)
    peer_rows = pl.ds(pl.multiple_of((1 - t) * half, half), half)
    front, back = pl.ds(0, width // 2), pl.ds(width // 2, width // 2)

    def x_copy(i):
        return send(snd_x.at[i], rcv_x.at[i], x_s.at[i], x_r.at[i], dev_x)

    def y_rows_copy(i):
        return send(snd_yr.at[i], rcv_yr.at[i], yr_s.at[i], yr_r.at[i], dev_y)

    def x_rows_copy(i):
        return send(snd_xr.at[i], rcv_xr.at[i], xr_s.at[i], xr_r.at[i], dev_x)

    def give_core_far(i, carry):
        snd_c[i] = down_chunk(chunk(z_turn(i), 1 - x, 1 - c)).astype(BF16)
        core_copy(i).start()
        return carry

    def give_core_near(i, carry):
        snd_c[4 + i] = down_chunk(chunk(z_turn(i), x, 1 - c)).astype(BF16)
        core_copy(4 + i).start()
        return carry

    def give_x(i, carry):
        own = down_chunk(chunk(z_turn(i), 1 - x, c))
        core_copy(i).wait_recv()
        acc[i] = own + rcv_c[i].astype(F32)
        snd_x[i] = acc[i, :, front].astype(BF16)
        x_copy(i).start()
        snd_yr[i] = acc[i, peer_rows, back].astype(BF16)
        y_rows_copy(i).start()
        return carry

    def keep(i, carry):
        own = down_chunk(chunk(z_turn(i), x, c))
        core_copy(4 + i).wait_recv()
        acc[4 + i] = own + rcv_c[4 + i].astype(F32)
        snd_yr[4 + i] = acc[4 + i, peer_rows, back].astype(BF16)
        y_rows_copy(4 + i).start()
        return carry

    def give_x_rows(i, carry):
        y_rows_copy(i).wait_recv()
        snd_xr[i] = (acc[i, my_rows, back] + rcv_yr[i].astype(F32)).astype(BF16)
        x_rows_copy(i).start()
        return carry

    def far_then_x(i, carry):
        return give_x(i - 1, give_core_far(i, carry))

    give_core_far(0, 0)
    lax.fori_loop(1, 4, far_then_x, 0)
    give_core_near(0, 0)
    give_x(3, 0)
    lax.fori_loop(1, 4, give_core_near, 0)
    lax.fori_loop(0, 4, keep, 0)
    lax.fori_loop(0, 4, give_x_rows, 0)

    def front_sum(i):
        x_copy(i).wait_recv()
        return acc[4 + i, :, front] + rcv_x[i].astype(F32)

    def back_sum(i):
        y_rows_copy(4 + i).wait_recv()
        x_rows_copy(i).wait_recv()
        return acc[4 + i, my_rows, back] + rcv_yr[4 + i].astype(F32) + rcv_xr[i].astype(F32)

    def to_z(src, dst, n, d):
        return start(send(src.at[d - 1], dst.at[d - 1], z_s.at[n], z_r.at[n], dev_z(d)))

    zs = []
    zrs = []
    for i, d in enumerate((2, 3, 1)):
        snd_z[d - 1] = front_sum(i).astype(BF16)
        zs.append(to_z(snd_z, rcv_z, d - 1, d))
    front_total = front_sum(3)
    for i, d in enumerate((2, 3, 1)):
        snd_zr[d - 1] = back_sum(i).astype(BF16)
        zrs.append(to_z(snd_zr, rcv_zr, 2 + d, d))
    back_total = back_sum(3)
    for copy, d in zip(zs, (2, 3, 1)):
        copy.wait_recv()
        front_total = front_total + rcv_z[d - 1].astype(F32)
    snd_y[...] = front_total.astype(BF16)
    fin = start(send(snd_y, rcv_y, y_s.at[0], y_r.at[0], dev_y))
    for copy, d in zip(zrs, (2, 3, 1)):
        copy.wait_recv()
        back_total = back_total + rcv_zr[d - 1].astype(F32)
    final[my_rows, :] = back_total.astype(BF16)
    fin_rows = start(send(final.at[my_rows], final.at[my_rows], y_s.at[1], y_r.at[1], dev_y))
    slot_rows = lax.broadcasted_iota(jnp.int32, (slots, live), 0) + t * slots
    live_lanes = lax.broadcasted_iota(jnp.int32, (slots, live), 1)
    place = jnp.where(slot_target(lengths, slot_rows, side) == live_lanes, 1.0, 0.0).astype(BF16)
    fin.wait_recv()
    front_part = (front_total + rcv_y[...].astype(F32)).astype(BF16)
    fin_rows.wait_recv()
    result = jnp.concatenate([front_part, final[...]], axis=1)
    out_ref[...] = jnp.dot(place, result, preferred_element_type=F32).astype(BF16)

    for copy in sent:
        copy.wait_send()
    for i in range(mine):
        gu_copy(i).wait_send()
        rate_copy(i).wait_send()
    for i in range(8):
        core_copy(i).wait_send()
        y_rows_copy(i).wait_send()
    for i in range(4):
        x_copy(i).wait_send()
        x_rows_copy(i).wait_send()


def local_kernel(
    tokens,
    seq_lengths,
    in_exponents,
    hidden_exponents,
    gateup_blocks,
    down_blocks,
    gate_values,
    up_values,
    down_values,
):
    slots, width = tokens.shape
    columns, kk, side, _ = gate_values.shape
    model_width = in_exponents.shape[0]
    blocks = model_width // side
    chunks = model_width // width
    mine = columns // 2
    t = lax.axis_index("tok")
    vmem = pl.BlockSpec(memory_space=pltpu.VMEM)
    anywhere = pl.BlockSpec(memory_space=pl.ANY)
    dma = lambda n: pltpu.SemaphoreType.DMA((n,))
    buf = lambda *shape: pltpu.VMEM(shape, BF16)
    return pl.pallas_call(
        body,
        out_shape=jax.ShapeDtypeStruct((slots, width), BF16),
        in_specs=[anywhere] * 9,
        out_specs=vmem,
        scratch_shapes=[
            pltpu.SMEM(seq_lengths.shape, jnp.int32),
            pltpu.SMEM(gateup_blocks.shape, jnp.int32),
            pltpu.VMEM(down_blocks.shape, jnp.int32),
            pltpu.VMEM((columns, 128), jnp.int32),
            pltpu.SMEM((columns, 128), jnp.int32),
            buf(slots, width),
            pltpu.VMEM((blocks, side), jnp.int32),
            pltpu.VMEM((columns, side), jnp.int32),
            buf(width, width),
            buf(columns, kk * side, side),
            buf(columns, kk * side, side),
            buf(columns, kk + 1, side, side),
            buf(slots, width),
            buf(chunks, slots, width),
            pltpu.VMEM((chunks, slots, width), F32),
            pltpu.VMEM((blocks, side), F32),
            buf(blocks, slots, side),
            buf(mine, slots, 2 * side),
            buf(mine, slots, 2 * side),
            buf(columns, slots, side),
            buf(8, slots, width),
            buf(8, slots, width),
            buf(4, slots, width // 2),
            buf(4, slots, width // 2),
            pltpu.VMEM((8, slots, width), F32),
            buf(slots, width // 2),
            buf(slots, width // 2),
            buf(3, slots, width // 2),
            buf(3, slots, width // 2),
            buf(8, slots // 2, width // 2),
            buf(8, slots // 2, width // 2),
            buf(4, slots // 2, width // 2),
            buf(4, slots // 2, width // 2),
            buf(3, slots // 2, width // 2),
            buf(3, slots // 2, width // 2),
            buf(slots, width // 2),
            dma(10),
            dma(1),
            dma(1),
            dma(3),
            dma(3),
            dma(4),
            dma(4),
            dma(8),
            dma(8),
            dma(mine),
            dma(mine),
            dma(mine),
            dma(mine),
            dma(8),
            dma(8),
            dma(4),
            dma(4),
            dma(2),
            dma(2),
            dma(6),
            dma(6),
            dma(8),
            dma(8),
            dma(4),
            dma(4),
        ],
        compiler_params=pltpu.CompilerParams(
            collective_id=0, has_side_effects=True, vmem_limit_bytes=60 * 1024 * 1024
        ),
        name="spiking_ffn",
    )(
        seq_lengths,
        gateup_blocks,
        down_blocks,
        tokens,
        in_exponents.reshape(blocks, side),
        hidden_exponents.reshape(columns, side),
        gate_values.reshape(columns, kk * side, side),
        up_values.reshape(columns, kk * side, side),
        down_values,
    )


def partner_2(value, axis, stride):
    mask = 2**stride
    pairs = [(source, source ^ mask) for source in range(lax.axis_size(axis))]
    return lax.ppermute(value, axis, pairs)


def sign_table(order_size, value_type):
    indices = jnp.arange(order_size, dtype=jnp.int32)
    shared = indices[:, None] & indices[None, :]
    parity = jnp.zeros((order_size, order_size), jnp.int32)
    for bit_number in range(max(1, (order_size - 1).bit_length())):
        parity = parity ^ shared >> bit_number & 1
    return (1 - 2 * parity).astype(value_type)


def local_general(
    tokens,
    seq_lengths,
    in_exponents,
    hidden_exponents,
    gateup_blocks,
    down_blocks,
    gate_values,
    up_values,
    down_values,
):
    slot_count, feat_local = tokens.shape
    model_width = in_exponents.shape[0]
    seq_width = slot_count // SEQS_DEV
    tok_index = lax.axis_index("tok")
    seq_count = seq_lengths.shape[0]
    earlier = jnp.tril(jnp.ones((seq_count, seq_count), jnp.int32))
    seq_ends = jnp.sum(earlier * seq_lengths[None, :], axis=1)
    seq_starts = seq_ends - seq_lengths
    seq_ids = jnp.arange(seq_lengths.shape[0], dtype=jnp.int32)
    slot_ids = jnp.arange(slot_count, dtype=jnp.int32)
    seq_of = tok_index * SEQS_DEV + slot_ids // seq_width
    position = slot_ids % seq_width
    same_seq = seq_of[:, None] == seq_ids[None, :]
    length_of = jnp.sum(jnp.where(same_seq, seq_lengths[None, :], 0), axis=1)
    start_of = jnp.sum(jnp.where(same_seq, seq_starts[None, :], 0), axis=1)
    live_slot = position < length_of
    pooled = lax.all_gather(tokens, "tok", axis=0, tiled=True)
    wanted = tok_index * seq_width + jnp.arange(seq_width, dtype=jnp.int32)
    owner_seq = jnp.sum((seq_ends[None, :] <= wanted[:, None]).astype(jnp.int32), axis=1)
    owner_match = owner_seq[:, None] == seq_ids[None, :]
    offset = wanted - jnp.sum(jnp.where(owner_match, seq_starts[None, :], 0), axis=1)
    picked_slot = owner_seq * seq_width + offset
    pooled_slots = jnp.arange(pooled.shape[0], dtype=jnp.int32)
    picker = (picked_slot[:, None] == pooled_slots[None, :]).astype(jnp.bfloat16)
    picked = jnp.dot(picker, pooled, preferred_element_type=jnp.float32).astype(jnp.bfloat16)
    row_count = picked.shape[0]
    rotation_scale = 1.0 / math.sqrt(model_width)
    mixed_part = jnp.dot(
        picked, sign_table(feat_local, jnp.bfloat16), preferred_element_type=jnp.float32
    )
    feat_index = lax.axis_index("feat")
    for bit_number in range(lax.axis_size("feat").bit_length() - 1):
        partner = partner_2(mixed_part, "feat", bit_number)
        high_half = feat_index >> bit_number & 1 == 1
        mixed_part = jnp.where(high_half, partner - mixed_part, mixed_part + partner)
    rotated = lax.all_gather(
        (mixed_part * rotation_scale).astype(jnp.bfloat16), "feat", axis=1, tiled=True
    )
    in_limit = jnp.exp2(in_exponents.astype(jnp.float32))
    hidden_limit = jnp.exp2(hidden_exponents.astype(jnp.float32))
    gate_full, up_full, down_full = (
        lax.all_gather(gate_values, "tok", axis=1, tiled=True),
        lax.all_gather(up_values, "tok", axis=1, tiled=True),
        lax.all_gather(down_values, "tok", axis=1, tiled=True),
    )
    block_size = gate_values.shape[2]
    block_count = model_width // block_size
    hidden_local = hidden_exponents.shape[0]
    spike_in = jnp.clip(rotated.astype(jnp.float32), -in_limit, in_limit).astype(jnp.bfloat16)
    block_ids = jnp.arange(block_count, dtype=jnp.int32)
    gateup_place = (gateup_blocks[:, :, None] == block_ids[None, None, :]).astype(jnp.bfloat16)

    def dense(values):
        wide = jnp.einsum(
            "hkbc,hkn->nbhc", values, gateup_place, preferred_element_type=jnp.float32
        )
        return wide.astype(jnp.bfloat16).reshape(model_width, hidden_local)

    gate_sum = jnp.dot(spike_in, dense(gate_full), preferred_element_type=jnp.float32)
    upward = jnp.dot(spike_in, dense(up_full), preferred_element_type=jnp.float32)
    current = jax.nn.silu(gate_sum) * upward
    spiking_rate = jnp.clip(current, -hidden_limit, hidden_limit).astype(jnp.bfloat16)
    indicator = (
        down_blocks[:, :, None] == jnp.arange(block_count, dtype=jnp.int32)[None, None, :]
    ).astype(jnp.bfloat16)
    dense_down_weight = jnp.einsum(
        "hkbc,hkn->hbnc", down_full, indicator, preferred_element_type=jnp.float32
    ).astype(jnp.bfloat16)
    dense_down_weight = dense_down_weight.reshape(hidden_local, model_width)
    partial_block_value = jnp.dot(
        spiking_rate, dense_down_weight, preferred_element_type=jnp.float32
    )
    summed = lax.psum_scatter(partial_block_value, "feat", scatter_dimension=1, tiled=True)
    returned = lax.all_gather(summed.astype(jnp.bfloat16), "tok", axis=0, tiled=True)
    source_row = jnp.where(live_slot, start_of + position, 0)
    returned_rows = jnp.arange(returned.shape[0], dtype=jnp.int32)
    placer = (source_row[:, None] == returned_rows[None, :]) & live_slot[:, None]
    return jnp.dot(
        placer.astype(jnp.bfloat16), returned, preferred_element_type=jnp.float32
    ).astype(jnp.bfloat16)


def solution(mesh):
    in_specs = (
        P("tok", "feat"),
        P(),
        P(),
        P("feat"),
        P("feat", None),
        P("feat", None),
        P("feat", "tok", None, None),
        P("feat", "tok", None, None),
        P("feat", "tok", None, None),
    )
    out_specs = P("tok", "feat")
    same_groups = dict(mesh.shape) == {"tok": 2, "feat": 16}
    local = local_kernel if same_groups else local_general
    return jax.shard_map(local, mesh=mesh, in_specs=in_specs, out_specs=out_specs, check_vma=False)
```
